512 devices in a mesh: row: 4 (over x), col: 16 (over z), depth: 8 (over y, core).
Axes of the slice: x: 4, y: 4, z: 16, core: 2. Of those that a mesh axis runs over, the one named last changes fastest.
Arguments:
- x_blocks: bfloat16 [16384, 8, 2048], P('col', 'depth', 'row'), may hold values from -0.5 to 0.5
- cols_x: int32 [16, 8, 16], P('col', 'depth'), may hold values from 0 to 95, as said below
- s_blocks: bfloat16 [8, 4096, 4, 1024], P('depth', 'col', 'row'), may hold values from -0.8984375 to 0.8984375
- rows_s: int32 [8, 4, 32], P('depth', 'row'), may hold values from 0 to 95, as said below
- keep_mask: int32 [128, 4, 8], P('col', 'row', 'depth'), may hold values 0 or 1
Outputs:
- filtered: bfloat16 [16384, 4, 1024], P('col', 'row', 'depth')
The draws below stay inside these ranges and needn't reach their ends.
Inputs may be any that keep to these rules, and one draw needn't show every extreme that they name: `cols_x`: within each list of 16 entries the numbers are distinct. `rows_s`: within each list of 32 entries the numbers are distinct.
All inputs are finite; a program needn't handle non-finite values. No bound on the sum of `keep_mask` on one device may be relied on, other than what follows from the above.
Results may differ from the reference program's by a relative error of at most 0.001.
Values may be sent and summed in bfloat16 or wider, within the bound.
A program may use at most 64 MiB of HBM per device.

```python
import jax
import jax.numpy as jnp

BS = 128
NB = 768
KBANDS = 8
JBANDS = 4
LX = 16
LS = 32
LK = 8
PANELS = 16
W = 128


def pool_starts(key):
    band_width = NB // KBANDS
    starts = jax.random.randint(key, (KBANDS,), 0, band_width).astype(jnp.int32)
    first = jnp.arange(KBANDS, dtype=jnp.int32) == 0
    return jnp.where(first, band_width - 1, starts).astype(jnp.int32)


def pooled_lists(key, starts, leading, count, forced):
    band_width = NB // KBANDS
    pool_width = min(40, band_width)
    scores = jax.random.randint(key, leading + (pool_width,), 0, 1 << 20) * pool_width
    offsets = jnp.arange(pool_width, dtype=jnp.int32)
    scores = scores + offsets
    scores = jnp.where(forced[..., None] & (offsets < 2), offsets - 2, scores)
    chosen = jnp.argsort(scores, axis=-1)[..., :count].astype(jnp.int32)
    return ((starts + chosen) % band_width).astype(jnp.int32)


def draw_cols_x(key, part):
    starts = pool_starts(key)
    key = jax.random.fold_in(key, 11)
    panel_ids = jnp.arange(PANELS, dtype=jnp.int32)[:, None]
    band_ids = jnp.arange(KBANDS, dtype=jnp.int32)[None, :]
    forced = (panel_ids == 0) & (band_ids == 0)
    return pooled_lists(key, starts[None, :, None], (PANELS, KBANDS), LX, forced)


def draw_rows_s(key, part):
    starts = pool_starts(key)
    key = jax.random.fold_in(key, 12)
    band_ids = jnp.arange(KBANDS, dtype=jnp.int32)[:, None]
    column_ids = jnp.arange(JBANDS, dtype=jnp.int32)[None, :]
    forced = (band_ids == 0) & (column_ids == 0)
    return pooled_lists(key, starts[:, None, None], (KBANDS, JBANDS), LS, forced)


def with_ends(array, own_key, low, top_value):
    extent = array.shape
    place = [jax.random.randint(jax.random.fold_in(own_key, axis), (), 0, extent[axis]) for axis in range(len(extent))]
    array = array.at[tuple(place)].set(low)
    longest = extent.index(max(extent))
    place[longest] = (place[longest] + 1) % extent[longest]
    return array.at[tuple(place)].set(top_value)


def raised(array, rng, source, target, blocks, factor):
    owner, partner = [(jnp.arange(array.shape[dim]) // (array.shape[dim] // blocks)).reshape([-1 if axis == dim else 1 for axis in range(array.ndim)]) for dim in (source, target)]
    chosen = jax.random.permutation(rng, blocks)[partner]
    strong = (owner == chosen) | (owner == (partner + blocks // 2) % blocks)
    return jnp.where(strong, factor * array, array)


def level_of(key, extent, pieces, low, high):
    def one(axis_at, parts):
        draws = jax.random.uniform(jax.random.fold_in(jax.random.fold_in(key, 6), axis_at), (parts,), jnp.float32, low / len(pieces), high / len(pieces))
        return jnp.repeat(jnp.exp(draws), extent[axis_at] // parts).reshape((-1,) + (1,) * (len(extent) - axis_at - 1))

    loudness = one(*pieces[0])
    for cut in pieces[1:]:
        loudness = loudness * one(*cut)
    return loudness


def centred(key, shape, width, reach, pieces=(), kind=jnp.bfloat16):
    result = jax.random.normal(key, shape, jnp.float32) * width
    if len(pieces) > 0:
        result = level_of(key, shape, pieces, -0.22, 0.18) * result
    return jnp.clip(result, min=-reach, max=reach).astype(kind)


def heavy_noise(stream_key, extent, width, limit, split, heavy, kind=jnp.bfloat16):
    drawn = width * jax.random.normal(stream_key, extent, jnp.float32)
    if split:
        drawn = drawn * level_of(stream_key, extent, split, -0.22, 0.18)
    return jnp.clip(raised(drawn, jax.random.fold_in(stream_key, 3), *heavy), -limit, limit).astype(kind)


def setup_inputs(seed: int = 0) -> dict:
    seeds = jax.random.split(jax.random.key(seed), 6)
    return {
        "x_blocks": centred(seeds[0], (W * BS, KBANDS, LX * BS), BS ** -0.5, 0.5, ((0, 16), (1, 8), (2, 4))),
        "cols_x": draw_cols_x(jax.random.fold_in(seeds[5], 71), 0),
        "s_blocks": heavy_noise(seeds[2], (KBANDS, LS * BS, JBANDS, LK * BS), 0.15, 0.8984375, ((0, 8), (1, 16), (2, 4)), (0, 3, 8, 2.0)),
        "rows_s": draw_rows_s(jax.random.fold_in(seeds[5], 71), 0),
        "keep_mask": with_ends((jax.random.randint(seeds[4], (W, JBANDS, LK), 0, 2) < 1).astype(jnp.int32), jax.random.fold_in(seeds[4], 1), 0, 1),
    }


def reference(x_blocks, cols_x, s_blocks, rows_s, keep_mask):
    panels = cols_x.shape[0]
    rows_panel = x_blocks.shape[0] // panels
    x_panels = x_blocks.reshape(panels, rows_panel, KBANDS, LX * BS)
    product = jax.vmap(lambda left, right: jnp.dot(left, right, preferred_element_type=jnp.float32))
    columns = []
    for j_band in range(JBANDS):
        partial_value = jnp.zeros((panels, rows_panel, LK * BS), jnp.float32)
        for k_band in range(KBANDS):
            s_rows = s_blocks[k_band, :, j_band, :].reshape(LS, BS, LK * BS)
            padded = jnp.concatenate([s_rows, jnp.zeros((1, BS, LK * BS), s_blocks.dtype)], axis=0)
            matches = cols_x[:, k_band, :, None] == rows_s[k_band, j_band][None, None, :]
            position = jnp.sum(jnp.where(matches, jnp.arange(LS, dtype=jnp.int32), 0), axis=2).astype(jnp.int32)
            position = position + jnp.where(jnp.any(matches, axis=2), 0, LS).astype(jnp.int32)
            picked = padded[position].reshape(panels, LX * BS, LK * BS)
            partial_value = partial_value + product(x_panels[:, :, k_band, :], picked)
        columns.append(partial_value)
    stacked = jnp.stack(columns, axis=2)
    window = panels * rows_panel // BS
    shaped = stacked.reshape(window, BS, JBANDS, LK, BS)
    filtered = jnp.where(keep_mask[:, None, :, :, None] > 0, shaped, 0.0)
    return filtered.reshape(window * BS, JBANDS, LK * BS).astype(jnp.bfloat16)
```

```python
import functools

import jax
import jax.numpy as jnp
from jax import lax
from jax.experimental import pallas as pl
from jax.experimental.pallas import tpu as pltpu
from jax.sharding import PartitionSpec as P

BS = 128
STAGGER = 4
X_FORWARD_SLOT = 10
X_READY_SLOT = 15
MESH = pl.DeviceIdType.MESH


def kernel(sizes, x_in, s_in, cols, rows, mask, out, s_buf, x_buf, cur, sel, oth, pair, total, red, pos,
           local_sem, s_send, s_recv, x_send, x_recv, p_send, p_recv, r_send, r_recv):
    ring, wide, deep = sizes
    half_ring = ring // 2
    width_x, width_s = cols.shape[0], rows.shape[0]
    chips = deep // 2
    z, r, d = lax.axis_index("col"), lax.axis_index("row"), lax.axis_index("depth")
    y, core = lax.div(d, 2), lax.rem(d, 2)
    quarter = x_in.shape[1]
    half = quarter // 2
    z_to = (lax.rem(z + 1, ring), lax.rem(z + ring - 1, ring))
    r_to = (lax.rem(r + 1, wide), lax.rem(r + wide - 1, wide))
    partner = 2 * y + 1 - core
    y_to = [lax.rem(y + 1 + j, chips) for j in range(chips)]

    barrier = pltpu.get_barrier_semaphore()
    friends = [{"col": z_to[0]}, {"col": z_to[1]}, {"row": r_to[0]}, {"row": r_to[1]}, {"depth": partner}]
    friends += [{"depth": 2 * y_to[j] + core} for j in range(chips - 1)]
    for friend in friends:
        pl.semaphore_signal(barrier, inc=1, device_id=friend, device_id_type=MESH)
    pl.semaphore_wait(barrier, len(friends))

    def tile_of(step):
        j, own = divmod(step, 2)
        return 2 * y_to[j] + (core if own else 1 - core)

    def s_copy(way, step, hop):
        back = (hop - 1) if way == 1 else (ring - hop + 1)
        block = lax.rem(z + back, ring)
        src = s_buf.at[step, block]
        if hop == 1:
            src = s_in.at[:, pl.ds(pl.multiple_of(tile_of(step) * BS, BS), BS)]
        dst = s_buf.at[step, block]
        if hop == half_ring:
            src, dst = src.at[pl.ds(way * BS, BS)], dst.at[pl.ds(way * BS, BS)]
        return pltpu.make_async_remote_copy(
            src_ref=src, dst_ref=dst, send_sem=s_send.at[way, step, hop - 1], recv_sem=s_recv.at[way, step, hop - 1],
            device_id={"col": z_to[way]}, device_id_type=MESH)

    def x_copy(way, piece):
        if piece < 2:
            part = piece if way == 0 else 1 - piece
            src = x_in.at[:, pl.ds(part * half, half)]
            owner = r
        else:
            part = way
            owner = r_to[1 - way]
        place = pl.ds(pl.multiple_of(owner * quarter + part * half, half), half)
        dst = x_buf.at[:, place]
        if piece == 2:
            src = dst
        return pltpu.make_async_remote_copy(
            src_ref=src, dst_ref=dst, send_sem=x_send.at[way, piece], recv_sem=x_recv.at[way, piece],
            device_id={"row": r_to[way]}, device_id_type=MESH)

    def p_copy(j):
        return pltpu.make_async_remote_copy(
            src_ref=oth.at[j], dst_ref=pair.at[j], send_sem=p_send.at[j], recv_sem=p_recv.at[j],
            device_id={"depth": partner}, device_id_type=MESH)

    def r_copy(j):
        return pltpu.make_async_remote_copy(
            src_ref=total.at[j], dst_ref=red.at[j], send_sem=r_send.at[j], recv_sem=r_recv.at[j],
            device_id={"depth": 2 * y_to[j] + core}, device_id_type=MESH)

    started = []

    def start(copy):
        copy.start()
        started.append(copy)

    for way in range(2):
        start(s_copy(way, 0, 1))
    for way in range(2):
        start(x_copy(way, 0))
    for way in range(2):
        start(x_copy(way, 1))
    locals_ = [pltpu.make_async_copy(x_in, x_buf.at[:, pl.ds(pl.multiple_of(r * quarter, quarter), quarter)], local_sem.at[0])]
    for step in range(deep):
        locals_.append(pltpu.make_async_copy(
            s_in.at[:, pl.ds(pl.multiple_of(tile_of(step) * BS, BS), BS)], s_buf.at[step, z], local_sem.at[1 + step]))
    for copy in locals_:
        copy.start()

    cur[width_s] = jnp.zeros((BS, BS), cur.dtype)

    def find(a, carry):
        wanted = cols[a]
        at = jnp.int32(width_s)
        for q in range(width_s):
            at = jnp.where(rows[q] == wanted, jnp.int32(q), at)
        pos[a] = at
        return carry

    lax.fori_loop(0, width_x, find, 0)
    for copy in locals_:
        copy.wait()

    tile_rows = 256

    def compute(step):
        j, own = divmod(step, 2)
        for q in range(width_s):
            cur[q] = s_buf[step, q // 2, pl.ds((q % 2) * BS, BS), :]

        def pick(a, carry):
            sel[pl.ds(pl.multiple_of(a * BS, BS), BS), :] = cur[pos[a]]
            return carry

        lax.fori_loop(0, width_x, pick, 0)
        if own:
            p_copy(j).wait_recv()
        if step == deep - 1:
            for k in range(chips - 1):
                r_copy(k).wait_recv()

        def tile(m, carry):
            here = pl.ds(pl.multiple_of(m * tile_rows, tile_rows), tile_rows)
            value = jnp.dot(x_buf[here, :], sel[...], preferred_element_type=jnp.float32)
            if not own:
                oth[j, here, :] = value
            elif step < deep - 1:
                total[j, here, :] = value + pair[j, here, :]
            else:
                value = value + pair[j, here, :]
                for k in range(chips - 1):
                    value = value + red[k, here, :]
                for part in range(tile_rows // BS):
                    keep = mask[m * (tile_rows // BS) + part] > 0
                    piece = value[part * BS:(part + 1) * BS]
                    to = pl.ds(pl.multiple_of(m * tile_rows + part * BS, BS), BS)
                    out[to, :] = jnp.where(keep, piece, 0.0).astype(out.dtype)
            return carry

        lax.fori_loop(0, x_buf.shape[0] // tile_rows, tile, 0)
        if not own:
            start(p_copy(j))
        elif step < deep - 1:
            start(r_copy(j))

    done = []
    slots = STAGGER * (deep - 1) + half_ring + 1
    for slot in range(slots):
        for step in range(deep):
            hop = slot - STAGGER * step + 1
            if hop < 1 or hop > half_ring + 1:
                continue
            for way in range(2):
                if hop > 1:
                    s_copy(way, step, hop - 1).wait_recv()
                if hop <= half_ring and (hop, step) != (1, 0):
                    start(s_copy(way, step, hop))
            if hop == half_ring + 1:
                done.append(step)
        if slot == X_FORWARD_SLOT:
            for way in range(2):
                x_copy(way, 0).wait_recv()
                start(x_copy(way, 2))
        if slot == X_READY_SLOT:
            for way in range(2):
                for piece in (1, 2):
                    x_copy(way, piece).wait_recv()
        if slot >= X_READY_SLOT and done:
            compute(done.pop(0))
    for step in done:
        compute(step)
    for copy in started:
        copy.wait_send()


def on_device(sizes, x_blocks, cols_x, s_blocks, rows_s, keep_mask):
    ring, wide, deep = sizes
    panel_rows, quarter = x_blocks.shape[0], x_blocks.shape[2]
    own_rows, kept = s_blocks.shape[1], s_blocks.shape[3]
    width_x, width_s = cols_x.shape[2], rows_s.shape[2]
    chips = deep // 2
    dma = pltpu.SemaphoreType.DMA
    smem = pl.BlockSpec(memory_space=pltpu.SMEM)
    anywhere = pl.BlockSpec(memory_space=pl.ANY)
    result = pl.pallas_call(
        functools.partial(kernel, sizes),
        out_shape=jax.ShapeDtypeStruct((panel_rows, BS), jnp.bfloat16),
        in_specs=[anywhere, anywhere, smem, smem, smem],
        out_specs=pl.BlockSpec(memory_space=pltpu.VMEM),
        scratch_shapes=[
            pltpu.VMEM((deep, ring, own_rows, BS), jnp.bfloat16),
            pltpu.VMEM((panel_rows, quarter * wide), jnp.bfloat16),
            pltpu.VMEM((width_s + 1, BS, BS), jnp.bfloat16),
            pltpu.VMEM((width_x * BS, BS), jnp.bfloat16),
            pltpu.VMEM((chips, panel_rows, BS), jnp.float32),
            pltpu.VMEM((chips, panel_rows, BS), jnp.float32),
            pltpu.VMEM((chips - 1, panel_rows, BS), jnp.float32),
            pltpu.VMEM((chips - 1, panel_rows, BS), jnp.float32),
            pltpu.SMEM((width_x,), jnp.int32),
            dma((1 + deep,)),
            dma((2, deep, ring // 2)),
            dma((2, deep, ring // 2)),
            dma((2, 3)),
            dma((2, 3)),
            dma((chips,)),
            dma((chips,)),
            dma((chips - 1,)),
            dma((chips - 1,)),
        ],
        compiler_params=pltpu.CompilerParams(collective_id=0, has_side_effects=True, vmem_limit_bytes=48 << 20),
    )(
        x_blocks.reshape(panel_rows, quarter),
        s_blocks.reshape(own_rows, kept),
        cols_x.reshape(width_x),
        rows_s.reshape(width_s),
        keep_mask.reshape(keep_mask.shape[0]),
    )
    return result.reshape(panel_rows, 1, BS)


def solution(mesh):
    sizes = (mesh.shape["col"], mesh.shape["row"], mesh.shape["depth"])
    placed = (
        P("col", "depth", "row"),
        P("col", "depth", None),
        P("depth", "col", "row", None),
        P("depth", "row", None),
        P("col", "row", "depth"),
    )
    return jax.shard_map(
        functools.partial(on_device, sizes), mesh=mesh, in_specs=placed, out_specs=P("col", "row", "depth"), check_vma=False
    )
```

```python
import functools

import jax
import jax.numpy as jnp
from jax import lax
from jax.experimental import pallas as pl
from jax.experimental.pallas import tpu as pltpu
from jax.sharding import PartitionSpec as P

BS = 128
TILE_ROWS = 512
MESH = pl.DeviceIdType.MESH


def send_order():
    order = [(pair, 1) for pair in range(4)]
    for hop in range(2, 6):
        order += [(0, hop), (1, hop)]
    for hop in range(6, 9):
        order += [(0, hop), (1, hop), (2, hop - 4)]
    for hop in range(5, 9):
        order += [(2, hop), (3, hop - 3)]
    order += [(3, hop) for hop in range(6, 9)]
    return order


WORK = {
    (1, 3): ["x_forward"],
    (1, 8): ["x_ready"],
    (3, 2): ["land 0", "pick 0", "dot 0 0"],
    (2, 6): ["dot 0 1"],
    (3, 3): ["land 1", "pick 1", "dot 1 0"],
    (2, 7): ["dot 1 1", "share 0"],
    (2, 8): ["share 1"],
    (3, 6): ["land 2", "pick 2", "dot 2 0", "dot 2 1"],
    (3, 7): ["share 2"],
    (3, 8): ["land 3", "pick 3", "dot 3 0", "dot 3 1", "finish"],
}


def kernel(sizes, x_in, s_in, cols, rows, mask, out, s_buf, x_buf, cur, sel, oth, own, pair_in, red, pos,
           local_sem, s_send, s_recv, x_send, x_recv, p_send, p_recv, r_send, r_recv):
    ring, wide, deep = sizes
    half_ring = ring // 2
    width_x, width_s = cols.shape[0], rows.shape[0]
    chips = deep // 2
    panel_rows = x_buf.shape[0]
    z, r, d = lax.axis_index("col"), lax.axis_index("row"), lax.axis_index("depth")
    y, core = lax.div(d, 2), lax.rem(d, 2)
    quarter = x_in.shape[1]
    half = quarter // 2
    z_to = (lax.rem(z + 1, ring), lax.rem(z + ring - 1, ring))
    r_to = (lax.rem(r + 1, wide), lax.rem(r + wide - 1, wide))
    partner = 2 * y + 1 - core

    barrier = pltpu.get_barrier_semaphore()
    friends = [{"col": z_to[0]}, {"col": z_to[1]}, {"row": r_to[0]}, {"row": r_to[1]}, {"depth": partner}]
    friends += [{"depth": 2 * lax.rem(y + j, chips) + core} for j in range(1, chips)]
    for friend in friends:
        pl.semaphore_signal(barrier, inc=1, device_id=friend, device_id_type=MESH)
    pl.semaphore_wait(barrier, len(friends))

    def tile_of(pair, side):
        which = core if side else 1 - core
        step = (2, 3 - 2 * which, 1 + 2 * which, 0)[pair]
        return 2 * lax.rem(y + step, chips) + which

    def columns(pair, side):
        return pl.ds(pl.multiple_of(tile_of(pair, side) * BS, BS), BS)

    def s_copy(way, pair, side, hop):
        back = (hop - 1) if way == 1 else (ring - hop + 1)
        block = lax.rem(z + back, ring)
        tile = 2 * pair + side
        dst = s_buf.at[tile, block]
        src = s_in.at[:, columns(pair, side)] if hop == 1 else dst
        if hop == half_ring:
            src, dst = src.at[pl.ds(way * BS, BS)], dst.at[pl.ds(way * BS, BS)]
        return pltpu.make_async_remote_copy(
            src_ref=src, dst_ref=dst, send_sem=s_send.at[way, tile, hop - 1], recv_sem=s_recv.at[way, tile, hop - 1],
            device_id={"col": z_to[way]}, device_id_type=MESH)

    def x_copy(way, piece):
        if piece < 2:
            part = piece if way == 0 else 1 - piece
            owner = r
        else:
            part = way
            owner = r_to[1 - way]
        dst = x_buf.at[:, pl.ds(pl.multiple_of(owner * quarter + part * half, half), half)]
        src = x_in.at[:, pl.ds(part * half, half)] if piece < 2 else dst
        return pltpu.make_async_remote_copy(
            src_ref=src, dst_ref=dst, send_sem=x_send.at[way, piece], recv_sem=x_recv.at[way, piece],
            device_id={"row": r_to[way]}, device_id_type=MESH)

    def p_copy(pair, part):
        here = pl.ds(part * TILE_ROWS, TILE_ROWS)
        return pltpu.make_async_remote_copy(
            src_ref=oth.at[pair, here], dst_ref=pair_in.at[pair, here], send_sem=p_send.at[pair, part],
            recv_sem=p_recv.at[pair, part], device_id={"depth": partner}, device_id_type=MESH)

    def r_copy(pair):
        return pltpu.make_async_remote_copy(
            src_ref=own.at[pair], dst_ref=red.at[pair], send_sem=r_send.at[pair], recv_sem=r_recv.at[pair],
            device_id={"depth": tile_of(pair, 1)}, device_id_type=MESH)

    started = []

    def start(copy):
        copy.start()
        started.append(copy)

    def advance(pair, hop):
        for side in range(2):
            for way in range(2):
                if hop > 1:
                    s_copy(way, pair, side, hop - 1).wait_recv()
                if hop <= half_ring:
                    start(s_copy(way, pair, side, hop))

    parts = panel_rows // TILE_ROWS

    def pick(pair):
        for side in range(2):
            for q in range(width_s):
                cur[side, q] = s_buf[2 * pair + side, q // 2, pl.ds((q % 2) * BS, BS), :]
        for a in range(width_x):
            at = pos[a]
            for side in range(2):
                sel[a * BS:(a + 1) * BS, side * BS:(side + 1) * BS] = cur[side, at]

    def dot(pair, part):
        here = pl.ds(part * TILE_ROWS, TILE_ROWS)
        value = jnp.dot(x_buf[here, :], sel[...], preferred_element_type=jnp.float32)
        oth[pair, here, :] = value[:, :BS]
        start(p_copy(pair, part))
        own[pair, here, :] = value[:, BS:]

    def share(pair):
        for part in range(parts):
            p_copy(pair, part).wait_recv()
        own[pair] = own[pair] + pair_in[pair]
        start(r_copy(pair))

    def finish():
        last = chips - 1
        for pair in range(last):
            r_copy(pair).wait_recv()
        for part in range(parts):
            p_copy(last, part).wait_recv()
        for i in range(panel_rows // BS):
            here = pl.ds(i * BS, BS)
            value = own[last, here, :] + pair_in[last, here, :]
            for pair in range(last):
                value = value + red[pair, here, :]
            out[here, :] = jnp.where(mask[i] > 0, value, 0.0).astype(out.dtype)

    def x_forward():
        for way in range(2):
            x_copy(way, 0).wait_recv()
            start(x_copy(way, 2))

    def x_ready():
        for way in range(2):
            for piece in (1, 2):
                x_copy(way, piece).wait_recv()

    local_copies = [pltpu.make_async_copy(
        x_in, x_buf.at[:, pl.ds(pl.multiple_of(r * quarter, quarter), quarter)], local_sem.at[0])]
    for pair in range(chips):
        for side in range(2):
            local_copies.append(pltpu.make_async_copy(
                s_in.at[:, columns(pair, side)], s_buf.at[2 * pair + side, z], local_sem.at[1 + 2 * pair + side]))

    def find(a, carry):
        wanted = cols[a]
        at = jnp.int32(width_s)
        for q in range(width_s):
            at = jnp.where(rows[q] == wanted, jnp.int32(q), at)
        pos[a] = at
        return carry

    order = send_order()
    for pair, hop in order[:1]:
        advance(pair, hop)
    for way in range(2):
        start(x_copy(way, 0))
    for pair, hop in order[1:chips]:
        advance(pair, hop)
    for way in range(2):
        start(x_copy(way, 1))
    for copy in local_copies:
        copy.start()
    for side in range(2):
        cur[side, width_s] = jnp.zeros((BS, BS), cur.dtype)
    lax.fori_loop(0, width_x, find, 0)
    for copy in local_copies:
        copy.wait()

    steps = {"x_forward": x_forward, "x_ready": x_ready, "pick": pick, "dot": dot, "share": share, "finish": finish,
             "land": lambda pair: advance(pair, half_ring + 1)}
    for pair, hop in order[chips:]:
        advance(pair, hop)
        for item in WORK.get((pair, hop), []):
            name, *numbers = item.split()
            steps[name](*map(int, numbers))
    for copy in started:
        copy.wait_send()


def on_device(sizes, x_blocks, cols_x, s_blocks, rows_s, keep_mask):
    ring, wide, deep = sizes
    panel_rows, quarter = x_blocks.shape[0], x_blocks.shape[2]
    own_rows, kept = s_blocks.shape[1], s_blocks.shape[3]
    width_x, width_s = cols_x.shape[2], rows_s.shape[2]
    chips = deep // 2
    parts = panel_rows // TILE_ROWS
    dma = pltpu.SemaphoreType.DMA
    smem = pl.BlockSpec(memory_space=pltpu.SMEM)
    anywhere = pl.BlockSpec(memory_space=pl.ANY)
    result = pl.pallas_call(
        functools.partial(kernel, sizes),
        out_shape=jax.ShapeDtypeStruct((panel_rows, BS), jnp.bfloat16),
        in_specs=[anywhere, anywhere, smem, smem, smem],
        out_specs=pl.BlockSpec(memory_space=pltpu.VMEM),
        scratch_shapes=[
            pltpu.VMEM((deep, ring, own_rows, BS), jnp.bfloat16),
            pltpu.VMEM((panel_rows, quarter * wide), jnp.bfloat16),
            pltpu.VMEM((2, width_s + 1, BS, BS), jnp.bfloat16),
            pltpu.VMEM((width_x * BS, 2 * BS), jnp.bfloat16),
            pltpu.VMEM((chips, panel_rows, BS), jnp.float32),
            pltpu.VMEM((chips, panel_rows, BS), jnp.float32),
            pltpu.VMEM((chips, panel_rows, BS), jnp.float32),
            pltpu.VMEM((chips - 1, panel_rows, BS), jnp.float32),
            pltpu.SMEM((width_x,), jnp.int32),
            dma((1 + deep,)),
            dma((2, deep, ring // 2)),
            dma((2, deep, ring // 2)),
            dma((2, 3)),
            dma((2, 3)),
            dma((chips, parts)),
            dma((chips, parts)),
            dma((chips - 1,)),
            dma((chips - 1,)),
        ],
        compiler_params=pltpu.CompilerParams(collective_id=0, has_side_effects=True, vmem_limit_bytes=60 << 20),
    )(
        x_blocks.reshape(panel_rows, quarter),
        s_blocks.reshape(own_rows, kept),
        cols_x.reshape(width_x),
        rows_s.reshape(width_s),
        keep_mask.reshape(keep_mask.shape[0]),
    )
    return result.reshape(panel_rows, 1, BS)


def solution(mesh):
    sizes = (mesh.shape["col"], mesh.shape["row"], mesh.shape["depth"])
    placed = (
        P("col", "depth", "row"),
        P("col", "depth", None),
        P("depth", "col", "row", None),
        P("depth", "row", None),
        P("col", "row", "depth"),
    )
    return jax.shard_map(
        functools.partial(on_device, sizes), mesh=mesh, in_specs=placed, out_specs=P("col", "row", "depth"), check_vma=False
    )
```

```python
import functools

import jax
import jax.numpy as jnp
from jax import lax
from jax.experimental import pallas as pl
from jax.experimental.pallas import tpu as pltpu
from jax.sharding import PartitionSpec as P

BS = 128
TILE_ROWS = 256
TRAIL = 2
MESH = pl.DeviceIdType.MESH


def send_order():
    order = [(pair, 1) for pair in range(4)]
    for hop in range(2, 9 - TRAIL):
        order += [(0, hop), (1, hop)]
    for hop in range(2, 2 + TRAIL):
        order += [(0, hop + 7 - TRAIL), (1, hop + 7 - TRAIL), (2, hop)]
    for hop in range(2 + TRAIL, 9):
        order += [(2, hop), (3, hop - TRAIL)]
    order += [(3, hop) for hop in range(9 - TRAIL, 9)]
    return order


WORK = {
    (1, 3): ["x_forward"],
    (1, 8): ["x_ready"],
    (3, 2): ["land 0", "pick 0", "dot 0 0 2"],
    (2, 5): ["dot 0 2 2"],
    (3, 3): ["land 1", "pick 1", "dot 1 0 2"],
    (2, 6): ["dot 1 2 2", "share 0"],
    (3, 4): ["share 1"],
    (2, 8): ["pick 2", "dot 2 0 2"],
    (3, 6): ["dot 2 2 2"],
    (3, 7): ["land 2", "late 2", "share 2"],
    (3, 8): ["pick 3", "dot 3 0 2", "dot 3 2 2", "land 3", "late 3", "finish"],
}


def kernel(sizes, x_in, s_in, cols, rows, mask, out, s_buf, x_buf, x_split, cur, sel, sel_last, oth, own, pair_in, red, pos, pos_last,
           local_sem, s_send, s_recv, x_send, x_recv, p_send, p_recv, r_send, r_recv):
    ring, wide, deep = sizes
    half_ring = ring // 2
    width_x, width_s = cols.shape[0], rows.shape[0]
    chips = deep // 2
    panel_rows = x_buf.shape[0]
    z, r, d = lax.axis_index("col"), lax.axis_index("row"), lax.axis_index("depth")
    y, core = lax.div(d, 2), lax.rem(d, 2)
    quarter = x_in.shape[1]
    half = quarter // 2
    z_to = (lax.rem(z + 1, ring), lax.rem(z + ring - 1, ring))
    r_to = (lax.rem(r + 1, wide), lax.rem(r + wide - 1, wide))
    partner = 2 * y + 1 - core

    barrier = pltpu.get_barrier_semaphore()
    friends = [{"col": z_to[0]}, {"col": z_to[1]}, {"row": r_to[0]}, {"row": r_to[1]}, {"depth": partner}]
    friends += [{"depth": 2 * lax.rem(y + j, chips) + core} for j in range(1, chips)]
    for friend in friends:
        pl.semaphore_signal(barrier, inc=1, device_id=friend, device_id_type=MESH)
    pl.semaphore_wait(barrier, len(friends))

    def tile_of(pair, side):
        which = core if side else 1 - core
        step = (2, 3 - 2 * which, 1 + 2 * which, 0)[pair]
        return 2 * lax.rem(y + step, chips) + which

    def columns(pair, side):
        return pl.ds(pl.multiple_of(tile_of(pair, side) * BS, BS), BS)

    def s_copy(way, pair, side, hop):
        back = (hop - 1) if way == 1 else (ring - hop + 1)
        block = lax.rem(z + back, ring)
        tile = 2 * pair + side
        dst = s_buf.at[tile, block]
        src = s_in.at[:, columns(pair, side)] if hop == 1 else dst
        if hop == half_ring:
            src, dst = src.at[pl.ds(way * BS, BS)], dst.at[pl.ds(way * BS, BS)]
        return pltpu.make_async_remote_copy(
            src_ref=src, dst_ref=dst, send_sem=s_send.at[way, tile, hop - 1], recv_sem=s_recv.at[way, tile, hop - 1],
            device_id={"col": z_to[way]}, device_id_type=MESH)

    def x_copy(way, piece):
        if piece < 2:
            part = piece if way == 0 else 1 - piece
            owner = r
        else:
            part = way
            owner = r_to[1 - way]
        dst = x_buf.at[:, pl.ds(pl.multiple_of(owner * quarter + part * half, half), half)]
        src = x_in.at[:, pl.ds(part * half, half)] if piece < 2 else dst
        return pltpu.make_async_remote_copy(
            src_ref=src, dst_ref=dst, send_sem=x_send.at[way, piece], recv_sem=x_recv.at[way, piece],
            device_id={"row": r_to[way]}, device_id_type=MESH)

    def p_copy(pair, part):
        here = pl.ds(part * TILE_ROWS, TILE_ROWS)
        return pltpu.make_async_remote_copy(
            src_ref=oth.at[pair, here], dst_ref=pair_in.at[pair, here], send_sem=p_send.at[pair, part],
            recv_sem=p_recv.at[pair, part], device_id={"depth": partner}, device_id_type=MESH)

    def r_copy(pair, part):
        here = pl.ds(part * TILE_ROWS, TILE_ROWS)
        return pltpu.make_async_remote_copy(
            src_ref=own.at[pair, here], dst_ref=red.at[pair, here], send_sem=r_send.at[pair, part],
            recv_sem=r_recv.at[pair, part], device_id={"depth": tile_of(pair, 1)}, device_id_type=MESH)

    started = []

    def start(copy):
        copy.start()
        started.append(copy)

    def advance(pair, hop):
        for side in range(2):
            for way in range(2):
                if hop > 1:
                    s_copy(way, pair, side, hop - 1).wait_recv()
                if hop <= half_ring:
                    start(s_copy(way, pair, side, hop))

    parts = panel_rows // TILE_ROWS
    last = chips - 1
    late_from = chips - 2
    far = lax.rem(z + half_ring, ring)

    def stage(pair, block):
        for side in range(2):
            for i in range(2):
                cur[side, 2 * block + i] = s_buf[2 * pair + side, block, pl.ds(i * BS, BS), :]

    def pick(pair):
        for back in range(ring):
            if pair >= late_from and back == half_ring:
                for side in range(2):
                    for i in range(2):
                        cur[side, 2 * far + i] = jnp.zeros((BS, BS), cur.dtype)
            else:
                stage(pair, lax.rem(z + back, ring))
        for a in range(width_x):
            at = pos[a]
            for side in range(2):
                sel[a * BS:(a + 1) * BS, side * BS:(side + 1) * BS] = cur[side, at]

    def dot(pair, part, count):
        here = pl.ds(part * TILE_ROWS, count * TILE_ROWS)
        value = jnp.dot(x_buf[here, :], sel[...], preferred_element_type=jnp.float32)
        oth[pair, here, :] = value[:, :BS]
        if pair < late_from:
            for k in range(part, part + count):
                start(p_copy(pair, k))
        own[pair, here, :] = value[:, BS:]

    def late(pair):
        stage(pair, far)
        for i in range(2):
            at = pos_last[2 + i]
            for side in range(2):
                sel_last[i * BS:(i + 1) * BS, side * BS:(side + 1) * BS] = cur[side, at]
        for part in range(parts):
            here = pl.ds(part * TILE_ROWS, TILE_ROWS)
            taken = [x_split[pos_last[i], here, :] for i in range(2)]
            value = jnp.dot(jnp.concatenate(taken, axis=1), sel_last[...], preferred_element_type=jnp.float32)
            oth[pair, here, :] = oth[pair, here, :] + value[:, :BS]
            start(p_copy(pair, part))
            own[pair, here, :] = own[pair, here, :] + value[:, BS:]

    def share(pair):
        for part in range(parts):
            here = pl.ds(part * TILE_ROWS, TILE_ROWS)
            p_copy(pair, part).wait_recv()
            own[pair, here, :] = own[pair, here, :] + pair_in[pair, here, :]
            start(r_copy(pair, part))

    def finish():
        for part in range(parts):
            for pair in range(last):
                r_copy(pair, part).wait_recv()
            p_copy(last, part).wait_recv()
            for i in range(part * TILE_ROWS // BS, (part + 1) * TILE_ROWS // BS):
                here = pl.ds(i * BS, BS)
                value = own[last, here, :] + pair_in[last, here, :]
                for pair in range(last):
                    value = value + red[pair, here, :]
                out[here, :] = jnp.where(mask[i] > 0, value, 0.0).astype(out.dtype)

    def x_forward():
        for way in range(2):
            x_copy(way, 0).wait_recv()
            start(x_copy(way, 2))

    def x_ready():
        for way in range(2):
            for piece in (1, 2):
                x_copy(way, piece).wait_recv()
        for a in range(width_x):
            x_split[a] = x_buf[:, a * BS:(a + 1) * BS]

    local_copies = [pltpu.make_async_copy(
        x_in, x_buf.at[:, pl.ds(pl.multiple_of(r * quarter, quarter), quarter)], local_sem.at[0])]
    for pair in range(chips):
        for side in range(2):
            local_copies.append(pltpu.make_async_copy(
                s_in.at[:, columns(pair, side)], s_buf.at[2 * pair + side, z], local_sem.at[1 + 2 * pair + side]))

    def find(a, carry):
        wanted = cols[a]
        at = jnp.int32(width_s)
        for q in range(width_s):
            at = jnp.where(rows[q] == wanted, jnp.int32(q), at)
        pos[a] = at
        return carry

    def find_last(i, carry):
        wanted = rows[2 * far + i]
        at_x, at_s = jnp.int32(0), jnp.int32(width_s)
        for a in range(width_x):
            same = cols[a] == wanted
            at_x = jnp.where(same, jnp.int32(a), at_x)
            at_s = jnp.where(same, 2 * far + i, at_s)
        pos_last[i] = at_x
        pos_last[2 + i] = at_s
        return carry

    order = send_order()
    for pair, hop in order[:1]:
        advance(pair, hop)
    for way in range(2):
        start(x_copy(way, 0))
    for pair, hop in order[1:chips]:
        advance(pair, hop)
    for way in range(2):
        start(x_copy(way, 1))
    for copy in local_copies:
        copy.start()
    for side in range(2):
        cur[side, width_s] = jnp.zeros((BS, BS), cur.dtype)
    lax.fori_loop(0, width_x, find, 0)
    lax.fori_loop(0, 2, find_last, 0)
    for copy in local_copies:
        copy.wait()

    steps = {"x_forward": x_forward, "x_ready": x_ready, "pick": pick, "dot": dot, "share": share, "late": late, "finish": finish,
             "land": lambda pair: advance(pair, half_ring + 1)}
    for pair, hop in order[chips:]:
        advance(pair, hop)
        for item in WORK.get((pair, hop), []):
            name, *numbers = item.split()
            steps[name](*map(int, numbers))
    for copy in started:
        copy.wait_send()


def on_device(sizes, x_blocks, cols_x, s_blocks, rows_s, keep_mask):
    ring, wide, deep = sizes
    panel_rows, quarter = x_blocks.shape[0], x_blocks.shape[2]
    own_rows, kept = s_blocks.shape[1], s_blocks.shape[3]
    width_x, width_s = cols_x.shape[2], rows_s.shape[2]
    chips = deep // 2
    parts = panel_rows // TILE_ROWS
    dma = pltpu.SemaphoreType.DMA
    smem = pl.BlockSpec(memory_space=pltpu.SMEM)
    anywhere = pl.BlockSpec(memory_space=pl.ANY)
    result = pl.pallas_call(
        functools.partial(kernel, sizes),
        out_shape=jax.ShapeDtypeStruct((panel_rows, BS), jnp.bfloat16),
        in_specs=[anywhere, anywhere, smem, smem, smem],
        out_specs=pl.BlockSpec(memory_space=pltpu.VMEM),
        scratch_shapes=[
            pltpu.VMEM((deep, ring, own_rows, BS), jnp.bfloat16),
            pltpu.VMEM((panel_rows, quarter * wide), jnp.bfloat16),
            pltpu.VMEM((width_x, panel_rows, BS), jnp.bfloat16),
            pltpu.VMEM((2, width_s + 1, BS, BS), jnp.bfloat16),
            pltpu.VMEM((width_x * BS, 2 * BS), jnp.bfloat16),
            pltpu.VMEM((2 * BS, 2 * BS), jnp.bfloat16),
            pltpu.VMEM((chips, panel_rows, BS), jnp.float32),
            pltpu.VMEM((chips, panel_rows, BS), jnp.float32),
            pltpu.VMEM((chips, panel_rows, BS), jnp.float32),
            pltpu.VMEM((chips - 1, panel_rows, BS), jnp.float32),
            pltpu.SMEM((width_x,), jnp.int32),
            pltpu.SMEM((4,), jnp.int32),
            dma((1 + deep,)),
            dma((2, deep, ring // 2)),
            dma((2, deep, ring // 2)),
            dma((2, 3)),
            dma((2, 3)),
            dma((chips, parts)),
            dma((chips, parts)),
            dma((chips - 1, parts)),
            dma((chips - 1, parts)),
        ],
        compiler_params=pltpu.CompilerParams(collective_id=0, has_side_effects=True, vmem_limit_bytes=213 << 18),
    )(
        x_blocks.reshape(panel_rows, quarter),
        s_blocks.reshape(own_rows, kept),
        cols_x.reshape(width_x),
        rows_s.reshape(width_s),
        keep_mask.reshape(keep_mask.shape[0]),
    )
    return result.reshape(panel_rows, 1, BS)


def solution(mesh):
    sizes = (mesh.shape["col"], mesh.shape["row"], mesh.shape["depth"])
    placed = (
        P("col", "depth", "row"),
        P("col", "depth", None),
        P("depth", "col", "row", None),
        P("depth", "row", None),
        P("col", "row", "depth"),
    )
    return jax.shard_map(
        functools.partial(on_device, sizes), mesh=mesh, in_specs=placed, out_specs=P("col", "row", "depth"), check_vma=False
    )
```

```python
import functools

import jax
import jax.numpy as jnp
from jax import lax
from jax.experimental import pallas as pl
from jax.experimental.pallas import tpu as pltpu
from jax.sharding import PartitionSpec as P

BS = 128
TILE_ROWS = 256
TRAIL = 1
MESH = pl.DeviceIdType.MESH


def send_order():
    order = [(pair, 1) for pair in range(4)]
    for hop in range(2, 9 - TRAIL):
        order += [(0, hop), (1, hop)]
    for hop in range(2, 2 + TRAIL):
        order += [(0, hop + 7 - TRAIL), (1, hop + 7 - TRAIL), (2, hop)]
    for hop in range(2 + TRAIL, 9):
        order += [(2, hop), (3, hop - TRAIL)]
    order += [(3, hop) for hop in range(9 - TRAIL, 9)]
    return order


WORK = {
    (1, 3): ["x_forward"],
    (1, 6): ["x_ready"],
    (3, 2): ["land 0", "pick 0", "dot 0 0 2"],
    (2, 4): ["dot 0 2 2"],
    (3, 3): ["land 1", "pick 1", "dot 1 0 2"],
    (2, 5): ["dot 1 2 2", "share 0 0 4"],
    (3, 4): ["share 1 0 4"],
    (2, 8): ["pick 2", "dot 2 0 2", "dot 2 2 2"],
    (3, 7): ["share 2 0 2", "land 2", "pass", "share 2 2 2"],
    (3, 8): ["pick 3", "dot 3 0 2", "dot 3 2 2", "land 3", "late", "take", "finish"],
}


def kernel(sizes, x_in, s_in, cols, rows, mask, out, s_buf, x_buf, x_split, x_far, x_far_in, s_far_in, cur, sel, sel_last, oth, own, pair_in,
           red, pos, pos_last,           local_sem, s_send, s_recv, x_send, x_recv, p_send, p_recv, r_send, r_recv,
           f_send, f_recv):
    ring, wide, deep = sizes
    half_ring = ring // 2
    width_x, width_s = cols.shape[0], rows.shape[0]
    chips = deep // 2
    panel_rows = x_buf.shape[0]
    z, r, d = lax.axis_index("col"), lax.axis_index("row"), lax.axis_index("depth")
    y, core = lax.div(d, 2), lax.rem(d, 2)
    quarter = x_in.shape[1]
    half = quarter // 2
    z_to = (lax.rem(z + 1, ring), lax.rem(z + ring - 1, ring))
    r_to = (lax.rem(r + 1, wide), lax.rem(r + wide - 1, wide))
    partner = 2 * y + 1 - core
    far = lax.rem(z + half_ring, ring)

    barrier = pltpu.get_barrier_semaphore()
    friends = [{"col": z_to[0]}, {"col": z_to[1]}, {"row": r_to[0]}, {"row": r_to[1]}, {"depth": partner}]
    friends += [{"depth": 2 * lax.rem(y + j, chips) + core} for j in range(1, chips)]
    beside = (2 * lax.rem(y + 1, chips), 2 * lax.rem(y + chips - 1, chips) + 1)
    friends.append({"depth": jnp.where(core == 0, beside[1], beside[0])})
    for friend in friends:
        pl.semaphore_signal(barrier, inc=1, device_id=friend, device_id_type=MESH)
    pl.semaphore_wait(barrier, len(friends))

    def tile_of(pair, side):
        which = core if side else 1 - core
        step = (2, 3 - 2 * which, 1 + 2 * which, 0)[pair]
        return 2 * lax.rem(y + step, chips) + which

    def columns(pair, side):
        return pl.ds(pl.multiple_of(tile_of(pair, side) * BS, BS), BS)

    def s_copy(way, pair, side, hop):
        back = (hop - 1) if way == 1 else (ring - hop + 1)
        block = lax.rem(z + back, ring)
        tile = 2 * pair + side
        dst = s_buf.at[tile, block]
        src = s_in.at[:, columns(pair, side)] if hop == 1 else dst
        if hop == half_ring:
            src, dst = src.at[pl.ds(way * BS, BS)], dst.at[pl.ds(way * BS, BS)]
        return pltpu.make_async_remote_copy(
            src_ref=src, dst_ref=dst, send_sem=s_send.at[way, tile, hop - 1], recv_sem=s_recv.at[way, tile, hop - 1],
            device_id={"col": z_to[way]}, device_id_type=MESH)

    def x_copy(way, piece):
        if piece < 2:
            part = piece if way == 0 else 1 - piece
            owner = r
        else:
            part = way
            owner = r_to[1 - way]
        dst = x_buf.at[:, pl.ds(pl.multiple_of(owner * quarter + part * half, half), half)]
        src = x_in.at[:, pl.ds(part * half, half)] if piece < 2 else dst
        return pltpu.make_async_remote_copy(
            src_ref=src, dst_ref=dst, send_sem=x_send.at[way, piece], recv_sem=x_recv.at[way, piece],
            device_id={"row": r_to[way]}, device_id_type=MESH)

    def p_copy(pair, part):
        here = pl.ds(part * TILE_ROWS, TILE_ROWS)
        return pltpu.make_async_remote_copy(
            src_ref=oth.at[pair, here], dst_ref=pair_in.at[pair, here], send_sem=p_send.at[pair, part],
            recv_sem=p_recv.at[pair, part], device_id={"depth": partner}, device_id_type=MESH)

    def r_copy(pair, part):
        here = pl.ds(part * TILE_ROWS, TILE_ROWS)
        return pltpu.make_async_remote_copy(
            src_ref=own.at[pair, here], dst_ref=red.at[pair, here], send_sem=r_send.at[pair, part],
            recv_sem=r_recv.at[pair, part], device_id={"depth": tile_of(pair, 1)}, device_id_type=MESH)

    def f_copy(which, sender, kind):
        side = jnp.where(core == which, 1, 0)
        src, dst = (x_far, x_far_in.at[sender]) if kind == 0 else (s_buf.at[4 + side, far], s_far_in.at[sender])
        return pltpu.make_async_remote_copy(
            src_ref=src, dst_ref=dst, send_sem=f_send.at[kind, which], recv_sem=f_recv.at[kind, sender],
            device_id={"depth": beside[which]}, device_id_type=MESH)

    started = []

    def start(copy):
        copy.start()
        started.append(copy)

    def advance(pair, hop):
        for side in range(2):
            for way in range(2):
                if hop > 1:
                    s_copy(way, pair, side, hop - 1).wait_recv()
                if hop <= half_ring:
                    start(s_copy(way, pair, side, hop))

    parts = panel_rows // TILE_ROWS
    last = chips - 1
    late_from = chips - 2

    def stage(pair, block):
        for side in range(2):
            for i in range(2):
                cur[side, 2 * block + i] = s_buf[2 * pair + side, block, pl.ds(i * BS, BS), :]

    def pick(pair):
        for back in range(ring):
            if pair >= late_from and back == half_ring:
                for side in range(2):
                    for i in range(2):
                        cur[side, 2 * far + i] = jnp.zeros((BS, BS), cur.dtype)
            else:
                stage(pair, lax.rem(z + back, ring))
        for a in range(width_x):
            at = pos[a]
            for side in range(2):
                sel[a * BS:(a + 1) * BS, side * BS:(side + 1) * BS] = cur[side, at]

    def dot(pair, part, count):
        here = pl.ds(part * TILE_ROWS, count * TILE_ROWS)
        value = jnp.dot(x_buf[here, :], sel[...], preferred_element_type=jnp.float32)
        oth[pair, here, :] = value[:, :BS]
        if pair != last:
            for k in range(part, part + count):
                start(p_copy(pair, k))
        own[pair, here, :] = value[:, BS:]

    def late():
        stage(last, far)
        for i in range(2):
            at = pos_last[2 + i]
            for side in range(2):
                sel_last[i * BS:(i + 1) * BS, side * BS:(side + 1) * BS] = cur[side, at]
        for part in range(parts):
            here = pl.ds(part * TILE_ROWS, TILE_ROWS)
            value = jnp.dot(x_far[here, :], sel_last[...], preferred_element_type=jnp.float32)
            oth[last, here, :] = oth[last, here, :] + value[:, :BS]
            start(p_copy(last, part))
            own[last, here, :] = own[last, here, :] + value[:, BS:]

    def pass_on():
        for which in range(2):
            start(f_copy(which, core, 1))

    def take():
        for kind in range(2):
            for sender in range(2):
                f_copy(0, sender, kind).wait_recv()
        for part in range(parts):
            here = pl.ds(part * TILE_ROWS, TILE_ROWS)
            value = own[last, here, :]
            for sender in range(2):
                value = value + jnp.dot(x_far_in[sender, here, :], s_far_in[sender], preferred_element_type=jnp.float32)
            own[last, here, :] = value

    def share(pair, first, count):
        for part in range(first, first + count):
            here = pl.ds(part * TILE_ROWS, TILE_ROWS)
            p_copy(pair, part).wait_recv()
            own[pair, here, :] = own[pair, here, :] + pair_in[pair, here, :]
            start(r_copy(pair, part))

    def finish():
        for part in range(parts):
            for pair in range(last):
                r_copy(pair, part).wait_recv()
            p_copy(last, part).wait_recv()
            for i in range(part * TILE_ROWS // BS, (part + 1) * TILE_ROWS // BS):
                here = pl.ds(i * BS, BS)
                value = own[last, here, :] + pair_in[last, here, :]
                for pair in range(last):
                    value = value + red[pair, here, :]
                out[here, :] = jnp.where(mask[i] > 0, value, 0.0).astype(out.dtype)

    def x_forward():
        for way in range(2):
            x_copy(way, 0).wait_recv()
            start(x_copy(way, 2))

    def x_ready():
        for way in range(2):
            for piece in (1, 2):
                x_copy(way, piece).wait_recv()
        for a in range(width_x):
            x_split[a] = x_buf[:, a * BS:(a + 1) * BS]
        x_split[width_x] = jnp.zeros((panel_rows, BS), x_split.dtype)
        for i in range(2):
            x_far[:, i * BS:(i + 1) * BS] = x_split[pos_last[i]]
        for which in range(2):
            start(f_copy(which, core, 0))

    local_copies = [pltpu.make_async_copy(
        x_in, x_buf.at[:, pl.ds(pl.multiple_of(r * quarter, quarter), quarter)], local_sem.at[0])]
    for pair in range(chips):
        for side in range(2):
            local_copies.append(pltpu.make_async_copy(
                s_in.at[:, columns(pair, side)], s_buf.at[2 * pair + side, z], local_sem.at[1 + 2 * pair + side]))

    def find(a, carry):
        wanted = cols[a]
        at = jnp.int32(width_s)
        for q in range(width_s):
            at = jnp.where(rows[q] == wanted, jnp.int32(q), at)
        pos[a] = at
        return carry

    def find_last(i, carry):
        wanted = rows[2 * far + i]
        at_x, at_s = jnp.int32(width_x), jnp.int32(width_s)
        for a in range(width_x):
            same = cols[a] == wanted
            at_x = jnp.where(same, jnp.int32(a), at_x)
            at_s = jnp.where(same, 2 * far + i, at_s)
        pos_last[i] = at_x
        pos_last[2 + i] = at_s
        return carry

    order = send_order()
    for pair, hop in order[:1]:
        advance(pair, hop)
    for way in range(2):
        start(x_copy(way, 0))
    for pair, hop in order[1:chips]:
        advance(pair, hop)
    for way in range(2):
        start(x_copy(way, 1))
    for copy in local_copies:
        copy.start()
    for side in range(2):
        cur[side, width_s] = jnp.zeros((BS, BS), cur.dtype)
    lax.fori_loop(0, width_x, find, 0)
    lax.fori_loop(0, 2, find_last, 0)
    for copy in local_copies:
        copy.wait()

    steps = {"x_forward": x_forward, "x_ready": x_ready, "pick": pick, "dot": dot, "share": share, "late": late, "pass": pass_on,
             "take": take, "finish": finish,
             "land": lambda pair: advance(pair, half_ring + 1)}
    for pair, hop in order[chips:]:
        advance(pair, hop)
        for item in WORK.get((pair, hop), []):
            name, *numbers = item.split()
            steps[name](*map(int, numbers))
    for copy in started:
        copy.wait_send()


def on_device(sizes, x_blocks, cols_x, s_blocks, rows_s, keep_mask):
    ring, wide, deep = sizes
    panel_rows, quarter = x_blocks.shape[0], x_blocks.shape[2]
    own_rows, kept = s_blocks.shape[1], s_blocks.shape[3]
    width_x, width_s = cols_x.shape[2], rows_s.shape[2]
    chips = deep // 2
    parts = panel_rows // TILE_ROWS
    dma = pltpu.SemaphoreType.DMA
    smem = pl.BlockSpec(memory_space=pltpu.SMEM)
    anywhere = pl.BlockSpec(memory_space=pl.ANY)
    result = pl.pallas_call(
        functools.partial(kernel, sizes),
        out_shape=jax.ShapeDtypeStruct((panel_rows, BS), jnp.bfloat16),
        in_specs=[anywhere, anywhere, smem, smem, smem],
        out_specs=pl.BlockSpec(memory_space=pltpu.VMEM),
        scratch_shapes=[
            pltpu.VMEM((deep, ring, own_rows, BS), jnp.bfloat16),
            pltpu.VMEM((panel_rows, quarter * wide), jnp.bfloat16),
            pltpu.VMEM((width_x + 1, panel_rows, BS), jnp.bfloat16),
            pltpu.VMEM((panel_rows, 2 * BS), jnp.bfloat16),
            pltpu.VMEM((2, panel_rows, 2 * BS), jnp.bfloat16),
            pltpu.VMEM((2, own_rows, BS), jnp.bfloat16),
            pltpu.VMEM((2, width_s + 1, BS, BS), jnp.bfloat16),
            pltpu.VMEM((width_x * BS, 2 * BS), jnp.bfloat16),
            pltpu.VMEM((2 * BS, 2 * BS), jnp.bfloat16),
            pltpu.VMEM((chips, panel_rows, BS), jnp.float32),
            pltpu.VMEM((chips, panel_rows, BS), jnp.float32),
            pltpu.VMEM((chips, panel_rows, BS), jnp.float32),
            pltpu.VMEM((chips - 1, panel_rows, BS), jnp.float32),
            pltpu.SMEM((width_x,), jnp.int32),
            pltpu.SMEM((4,), jnp.int32),
            dma((1 + deep,)),
            dma((2, deep, ring // 2)),
            dma((2, deep, ring // 2)),
            dma((2, 3)),
            dma((2, 3)),
            dma((chips, parts)),
            dma((chips, parts)),
            dma((chips - 1, parts)),
            dma((chips - 1, parts)),
            dma((2, 2)),
            dma((2, 2)),
        ],
        compiler_params=pltpu.CompilerParams(collective_id=0, has_side_effects=True, vmem_limit_bytes=213 << 18),
    )(
        x_blocks.reshape(panel_rows, quarter),
        s_blocks.reshape(own_rows, kept),
        cols_x.reshape(width_x),
        rows_s.reshape(width_s),
        keep_mask.reshape(keep_mask.shape[0]),
    )
    return result.reshape(panel_rows, 1, BS)


def solution(mesh):
    sizes = (mesh.shape["col"], mesh.shape["row"], mesh.shape["depth"])
    placed = (
        P("col", "depth", "row"),
        P("col", "depth", None),
        P("depth", "col", "row", None),
        P("depth", "row", None),
        P("col", "row", "depth"),
    )
    return jax.shard_map(
        functools.partial(on_device, sizes), mesh=mesh, in_specs=placed, out_specs=P("col", "row", "depth"), check_vma=False
    )
```

```python
import functools

import jax
import jax.numpy as jnp
from jax import lax
from jax.experimental import pallas as pl
from jax.experimental.pallas import tpu as pltpu
from jax.sharding import PartitionSpec as P

BS = 128
TILE_ROWS = 256
TRAIL = 1
MESH = pl.DeviceIdType.MESH


def send_order():
    order = [(pair, 1) for pair in range(4)]
    for hop in range(2, 9 - TRAIL):
        order += [(0, hop), (1, hop)]
    for hop in range(2, 2 + TRAIL):
        order += [(0, hop + 7 - TRAIL), (1, hop + 7 - TRAIL), (2, hop)]
    for hop in range(2 + TRAIL, 9):
        order += [(2, hop), (3, hop - TRAIL)]
    order += [(3, hop) for hop in range(9 - TRAIL, 9)]
    return order


WORK = {
    (1, 3): ["x_forward"],
    (1, 6): ["x_ready"],
    (3, 2): ["land 0", "pick 0", "dot 0 0 2"],
    (2, 4): ["dot 0 2 2"],
    (3, 3): ["land 1", "pick 1", "dot 1 0 2"],
    (2, 5): ["dot 1 2 2", "share 0 0 4"],
    (3, 4): ["share 1 0 4"],
    (2, 8): ["pick 2", "dot 2 0 2", "dot 2 2 2"],
    (3, 7): ["share 2 0 2", "land 2", "pass", "share 2 2 2"],
    (3, 8): ["pick 3", "dot 3 0 2", "dot 3 2 2", "land 3", "late", "take", "finish"],
}


def kernel(sizes, x_in, s_in, cols_in, rows_in, mask_in, out, cols, rows, mask, s_buf, x_buf, x_split, x_far, x_far_in, s_far_in, cur, sel, oth, own, pair_in,
           red, pos, pos_far,           local_sem, s_send, s_recv, x_send, x_recv, p_send, p_recv, r_send, r_recv,
           f_send, f_recv):
    ring, wide, deep = sizes
    half_ring = ring // 2
    width_x, width_s = cols.shape[0], rows.shape[0]
    chips = deep // 2
    panel_rows = x_buf.shape[0]
    z, r, d = lax.axis_index("col"), lax.axis_index("row"), lax.axis_index("depth")
    y, core = lax.div(d, 2), lax.rem(d, 2)
    quarter = x_in.shape[1]
    half = quarter // 2
    z_to = (lax.rem(z + 1, ring), lax.rem(z + ring - 1, ring))
    r_to = (lax.rem(r + 1, wide), lax.rem(r + wide - 1, wide))
    partner = 2 * y + 1 - core
    far = lax.rem(z + half_ring, ring)

    barrier = pltpu.get_barrier_semaphore()
    friends = [{"col": z_to[0]}, {"col": z_to[1]}, {"row": r_to[0]}, {"row": r_to[1]}, {"depth": partner}]
    friends += [{"depth": 2 * lax.rem(y + j, chips) + core} for j in range(1, chips)]
    beside = (2 * lax.rem(y + 1, chips), 2 * lax.rem(y + chips - 1, chips) + 1)
    friends.append({"depth": jnp.where(core == 0, beside[1], beside[0])})
    for friend in friends:
        pl.semaphore_signal(barrier, inc=1, device_id=friend, device_id_type=MESH)
    pl.semaphore_wait(barrier, len(friends))

    def tile_of(pair, side):
        which = core if side else 1 - core
        step = (2, 3 - 2 * which, 1 + 2 * which, 0)[pair]
        return 2 * lax.rem(y + step, chips) + which

    def columns(pair, side):
        return pl.ds(pl.multiple_of(tile_of(pair, side) * BS, BS), BS)

    def s_copy(way, pair, side, hop):
        back = (hop - 1) if way == 1 else (ring - hop + 1)
        block = lax.rem(z + back, ring)
        tile = 2 * pair + side
        dst = s_buf.at[tile, block]
        src = s_in.at[:, columns(pair, side)] if hop == 1 else dst
        if hop == half_ring:
            src, dst = src.at[pl.ds(way * BS, BS)], dst.at[pl.ds(way * BS, BS)]
        return pltpu.make_async_remote_copy(
            src_ref=src, dst_ref=dst, send_sem=s_send.at[way, tile, hop - 1], recv_sem=s_recv.at[way, tile, hop - 1],
            device_id={"col": z_to[way]}, device_id_type=MESH)

    def x_copy(way, piece):
        if piece < 2:
            part = piece if way == 0 else 1 - piece
            owner = r
        else:
            part = way
            owner = r_to[1 - way]
        dst = x_buf.at[:, pl.ds(pl.multiple_of(owner * quarter + part * half, half), half)]
        src = x_in.at[:, pl.ds(part * half, half)] if piece < 2 else dst
        return pltpu.make_async_remote_copy(
            src_ref=src, dst_ref=dst, send_sem=x_send.at[way, piece], recv_sem=x_recv.at[way, piece],
            device_id={"row": r_to[way]}, device_id_type=MESH)

    def p_copy(pair, part):
        here = pl.ds(part * TILE_ROWS, TILE_ROWS)
        return pltpu.make_async_remote_copy(
            src_ref=oth.at[pair, here], dst_ref=pair_in.at[pair, here], send_sem=p_send.at[pair, part],
            recv_sem=p_recv.at[pair, part], device_id={"depth": partner}, device_id_type=MESH)

    def r_copy(pair, part):
        here = pl.ds(part * TILE_ROWS, TILE_ROWS)
        return pltpu.make_async_remote_copy(
            src_ref=own.at[pair, here], dst_ref=red.at[pair, here], send_sem=r_send.at[pair, part],
            recv_sem=r_recv.at[pair, part], device_id={"depth": tile_of(pair, 1)}, device_id_type=MESH)

    def f_copy(which, sender, kind):
        side = jnp.where(core == which, 1, 0)
        place = pl.ds(pl.multiple_of(sender * 2 * BS, 2 * BS), 2 * BS)
        src, dst = (x_far, x_far_in.at[:, place]) if kind == 0 else (s_buf.at[4 + side, far], s_far_in.at[place])
        return pltpu.make_async_remote_copy(
            src_ref=src, dst_ref=dst, send_sem=f_send.at[kind, which], recv_sem=f_recv.at[kind, sender],
            device_id={"depth": beside[which]}, device_id_type=MESH)

    started = []

    def start(copy):
        copy.start()
        started.append(copy)

    def advance(pair, hop):
        for side in range(2):
            for way in range(2):
                if hop > 1:
                    s_copy(way, pair, side, hop - 1).wait_recv()
                if hop <= half_ring:
                    start(s_copy(way, pair, side, hop))

    parts = panel_rows // TILE_ROWS
    last = chips - 1
    late_from = chips - 2

    def stage(pair, block):
        for side in range(2):
            for i in range(2):
                cur[side, 2 * block + i] = s_buf[2 * pair + side, block, pl.ds(i * BS, BS), :]

    def pick(pair):
        for back in range(ring):
            if pair >= late_from and back == half_ring:
                for side in range(2):
                    for i in range(2):
                        cur[side, 2 * far + i] = jnp.zeros((BS, BS), cur.dtype)
            else:
                stage(pair, lax.rem(z + back, ring))
        for a in range(width_x):
            at = pos[a]
            for side in range(2):
                sel[a * BS:(a + 1) * BS, side * BS:(side + 1) * BS] = cur[side, at]

    def dot(pair, part, count):
        here = pl.ds(part * TILE_ROWS, count * TILE_ROWS)
        value = jnp.dot(x_buf[here, :], sel[...], preferred_element_type=jnp.float32)
        oth[pair, here, :] = value[:, :BS]
        if pair != last:
            for k in range(part, part + count):
                start(p_copy(pair, k))
        own[pair, here, :] = value[:, BS:]

    def late():
        rows_far = jnp.concatenate([s_buf[2 * last, far], s_buf[2 * last + 1, far]], axis=1)
        for part in range(parts):
            here = pl.ds(part * TILE_ROWS, TILE_ROWS)
            value = jnp.dot(x_far[here, :], rows_far, preferred_element_type=jnp.float32)
            oth[last, here, :] = oth[last, here, :] + value[:, :BS]
            start(p_copy(last, part))
            own[last, here, :] = own[last, here, :] + value[:, BS:]

    def pass_on():
        for which in range(2):
            start(f_copy(which, core, 1))

    def take():
        for kind in range(2):
            for sender in range(2):
                f_copy(0, sender, kind).wait_recv()
        for part in range(0, parts, 2):
            here = pl.ds(part * TILE_ROWS, 2 * TILE_ROWS)
            value = jnp.dot(x_far_in[here, :], s_far_in[...], preferred_element_type=jnp.float32)
            own[last, here, :] = own[last, here, :] + value

    def share(pair, first, count):
        for part in range(first, first + count):
            here = pl.ds(part * TILE_ROWS, TILE_ROWS)
            p_copy(pair, part).wait_recv()
            own[pair, here, :] = own[pair, here, :] + pair_in[pair, here, :]
            start(r_copy(pair, part))

    def finish():
        for part in range(parts):
            for pair in range(last):
                r_copy(pair, part).wait_recv()
            p_copy(last, part).wait_recv()
            for i in range(part * TILE_ROWS // BS, (part + 1) * TILE_ROWS // BS):
                here = pl.ds(i * BS, BS)
                value = own[last, here, :] + pair_in[last, here, :]
                for pair in range(last):
                    value = value + red[pair, here, :]
                out[here, :] = jnp.where(mask[i] > 0, value, 0.0).astype(out.dtype)

    def x_forward():
        for way in range(2):
            x_copy(way, 0).wait_recv()
            start(x_copy(way, 2))

    def x_ready():
        for way in range(2):
            for piece in (1, 2):
                x_copy(way, piece).wait_recv()
        for a in range(width_x):
            x_split[a] = x_buf[:, a * BS:(a + 1) * BS]
        x_split[width_x] = jnp.zeros((panel_rows, BS), x_split.dtype)
        for i in range(2):
            x_far[:, i * BS:(i + 1) * BS] = x_split[pos_far[i]]
        for which in range(2):
            start(f_copy(which, core, 0))

    local_copies = [pltpu.make_async_copy(
        x_in, x_buf.at[:, pl.ds(pl.multiple_of(r * quarter, quarter), quarter)], local_sem.at[0])]
    for pair in range(chips):
        for side in range(2):
            local_copies.append(pltpu.make_async_copy(
                s_in.at[:, columns(pair, side)], s_buf.at[2 * pair + side, z], local_sem.at[1 + 2 * pair + side]))

    for k, (src, dst) in enumerate(((cols_in, cols), (rows_in, rows), (mask_in, mask))):
        local_copies.append(pltpu.make_async_copy(src, dst, local_sem.at[1 + deep + k]))

    def find(a, carry):
        wanted = cols[a]
        at = jnp.int32(width_s)
        for q in range(width_s):
            at = jnp.where(rows[q] == wanted, jnp.int32(q), at)
        pos[a] = at
        return carry

    def find_far(i, carry):
        wanted = rows[2 * far + i]
        at = jnp.int32(width_x)
        for a in range(width_x):
            at = jnp.where(cols[a] == wanted, jnp.int32(a), at)
        pos_far[i] = at
        return carry

    order = send_order()
    for pair, hop in order[:1]:
        advance(pair, hop)
    for way in range(2):
        start(x_copy(way, 0))
    for pair, hop in order[1:chips]:
        advance(pair, hop)
    for way in range(2):
        start(x_copy(way, 1))
    for copy in local_copies:
        copy.start()
    for side in range(2):
        cur[side, width_s] = jnp.zeros((BS, BS), cur.dtype)
    for copy in local_copies:
        copy.wait()
    lax.fori_loop(0, width_x, find, 0)
    lax.fori_loop(0, 2, find_far, 0)

    steps = {"x_forward": x_forward, "x_ready": x_ready, "pick": pick, "dot": dot, "share": share, "late": late, "pass": pass_on,
             "take": take, "finish": finish,
             "land": lambda pair: advance(pair, half_ring + 1)}
    for pair, hop in order[chips:]:
        advance(pair, hop)
        for item in WORK.get((pair, hop), []):
            name, *numbers = item.split()
            steps[name](*map(int, numbers))
    for copy in started:
        copy.wait_send()


def on_device(sizes, x_blocks, cols_x, s_blocks, rows_s, keep_mask):
    ring, wide, deep = sizes
    panel_rows, quarter = x_blocks.shape[0], x_blocks.shape[2]
    own_rows, kept = s_blocks.shape[1], s_blocks.shape[3]
    width_x, width_s = cols_x.shape[2], rows_s.shape[2]
    chips = deep // 2
    parts = panel_rows // TILE_ROWS
    dma = pltpu.SemaphoreType.DMA
    anywhere = pl.BlockSpec(memory_space=pl.ANY)
    result = pl.pallas_call(
        functools.partial(kernel, sizes),
        out_shape=jax.ShapeDtypeStruct((panel_rows, BS), jnp.bfloat16),
        in_specs=[anywhere] * 5,
        out_specs=pl.BlockSpec(memory_space=pltpu.VMEM),
        scratch_shapes=[
            pltpu.SMEM((width_x,), jnp.int32),
            pltpu.SMEM((width_s,), jnp.int32),
            pltpu.SMEM((keep_mask.shape[0],), jnp.int32),
            pltpu.VMEM((deep, ring, own_rows, BS), jnp.bfloat16),
            pltpu.VMEM((panel_rows, quarter * wide), jnp.bfloat16),
            pltpu.VMEM((width_x + 1, panel_rows, BS), jnp.bfloat16),
            pltpu.VMEM((panel_rows, 2 * BS), jnp.bfloat16),
            pltpu.VMEM((panel_rows, 4 * BS), jnp.bfloat16),
            pltpu.VMEM((4 * BS, BS), jnp.bfloat16),
            pltpu.VMEM((2, width_s + 1, BS, BS), jnp.bfloat16),
            pltpu.VMEM((width_x * BS, 2 * BS), jnp.bfloat16),
            pltpu.VMEM((chips, panel_rows, BS), jnp.float32),
            pltpu.VMEM((chips, panel_rows, BS), jnp.float32),
            pltpu.VMEM((chips, panel_rows, BS), jnp.float32),
            pltpu.VMEM((chips - 1, panel_rows, BS), jnp.float32),
            pltpu.SMEM((width_x,), jnp.int32),
            pltpu.SMEM((2,), jnp.int32),
            dma((4 + deep,)),
            dma((2, deep, ring // 2)),
            dma((2, deep, ring // 2)),
            dma((2, 3)),
            dma((2, 3)),
            dma((chips, parts)),
            dma((chips, parts)),
            dma((chips - 1, parts)),
            dma((chips - 1, parts)),
            dma((2, 2)),
            dma((2, 2)),
        ],
        compiler_params=pltpu.CompilerParams(collective_id=0, has_side_effects=True, vmem_limit_bytes=213 << 18),
    )(
        x_blocks.reshape(panel_rows, quarter),
        s_blocks.reshape(own_rows, kept),
        cols_x.reshape(width_x),
        rows_s.reshape(width_s),
        keep_mask.reshape(keep_mask.shape[0]),
    )
    return result.reshape(panel_rows, 1, BS)


def solution(mesh):
    sizes = (mesh.shape["col"], mesh.shape["row"], mesh.shape["depth"])
    placed = (
        P("col", "depth", "row"),
        P("col", "depth", None),
        P("depth", "col", "row", None),
        P("depth", "row", None),
        P("col", "row", "depth"),
    )
    return jax.shard_map(
        functools.partial(on_device, sizes), mesh=mesh, in_specs=placed, out_specs=P("col", "row", "depth"), check_vma=False
    )
```

```python
import functools

import jax
import jax.numpy as jnp
from jax import lax
from jax.experimental import pallas as pl
from jax.experimental.pallas import tpu as pltpu
from jax.sharding import PartitionSpec as P

BS = 128
TILE_ROWS = 256
TRAIL = 1
MESH = pl.DeviceIdType.MESH


def send_order():
    order = [(pair, 1) for pair in range(4)]
    for hop in range(2, 9 - TRAIL):
        order += [(0, hop), (1, hop)]
    for hop in range(2, 2 + TRAIL):
        order += [(0, hop + 7 - TRAIL), (1, hop + 7 - TRAIL), (2, hop)]
    for hop in range(2 + TRAIL, 9):
        order += [(2, hop), (3, hop - TRAIL)]
    order += [(3, hop) for hop in range(9 - TRAIL, 9)]
    return order


WORK = {
    (1, 4): ["x_forward"],
    (1, 7): ["x_ready"],
    (3, 2): ["land 0", "pick 0", "dot 0 0 2"],
    (2, 4): ["dot 0 2 2"],
    (3, 3): ["land 1", "pick 1", "dot 1 0 2"],
    (2, 5): ["dot 1 2 2", "share 0 0 4"],
    (3, 4): ["share 1 0 4"],
    (2, 8): ["pick 2", "dot 2 0 2", "dot 2 2 2"],
    (3, 7): ["share 2 0 2", "land 2", "pass", "share 2 2 2"],
    (3, 8): ["pick 3", "dot 3 0 2", "dot 3 2 2", "gather", "land 3", "late", "take", "finish"],
}


def kernel(sizes, x_in, s_in, cols_in, rows_in, mask_in, out, cols, rows, mask, s_buf, x_buf, x_split, x_far, x_far_in, s_far_in, cur, sel, oth, own, pair_in,
           red, pos, pos_far,           local_sem, s_send, s_recv, x_send, x_recv, p_send, p_recv, r_send, r_recv,
           f_send, f_recv):
    ring, wide, deep = sizes
    half_ring = ring // 2
    width_x, width_s = cols.shape[0], rows.shape[0]
    chips = deep // 2
    panel_rows = x_buf.shape[0]
    z, r, d = lax.axis_index("col"), lax.axis_index("row"), lax.axis_index("depth")
    y, core = lax.div(d, 2), lax.rem(d, 2)
    quarter = x_in.shape[1]
    half = quarter // 2
    z_to = (lax.rem(z + 1, ring), lax.rem(z + ring - 1, ring))
    r_to = (lax.rem(r + 1, wide), lax.rem(r + wide - 1, wide))
    partner = 2 * y + 1 - core
    far = lax.rem(z + half_ring, ring)

    barrier = pltpu.get_barrier_semaphore()
    friends = [{"col": z_to[0]}, {"col": z_to[1]}, {"row": r_to[0]}, {"row": r_to[1]}, {"depth": partner}]
    friends += [{"depth": 2 * lax.rem(y + j, chips) + core} for j in range(1, chips)]
    beside = (2 * lax.rem(y + 1, chips), 2 * lax.rem(y + chips - 1, chips) + 1)
    friends.append({"depth": jnp.where(core == 0, beside[1], beside[0])})
    for friend in friends:
        pl.semaphore_signal(barrier, inc=1, device_id=friend, device_id_type=MESH)
    pl.semaphore_wait(barrier, len(friends))

    def tile_of(pair, side):
        which = core if side else 1 - core
        step = (2, 3 - 2 * which, 1 + 2 * which, 0)[pair]
        return 2 * lax.rem(y + step, chips) + which

    def columns(pair, side):
        return pl.ds(pl.multiple_of(tile_of(pair, side) * BS, BS), BS)

    def s_copy(way, pair, side, hop):
        back = (hop - 1) if way == 1 else (ring - hop + 1)
        block = lax.rem(z + back, ring)
        tile = 2 * pair + side
        dst = s_buf.at[tile, block]
        src = s_in.at[:, columns(pair, side)] if hop == 1 else dst
        if hop == half_ring:
            src, dst = src.at[pl.ds(way * BS, BS)], dst.at[pl.ds(way * BS, BS)]
        return pltpu.make_async_remote_copy(
            src_ref=src, dst_ref=dst, send_sem=s_send.at[way, tile, hop - 1], recv_sem=s_recv.at[way, tile, hop - 1],
            device_id={"col": z_to[way]}, device_id_type=MESH)

    def x_copy(way, piece):
        if piece < 2:
            part = piece if way == 0 else 1 - piece
            owner = r
        else:
            part = way
            owner = r_to[1 - way]
        dst = x_buf.at[:, pl.ds(pl.multiple_of(owner * quarter + part * half, half), half)]
        src = x_in.at[:, pl.ds(part * half, half)] if piece < 2 else dst
        return pltpu.make_async_remote_copy(
            src_ref=src, dst_ref=dst, send_sem=x_send.at[way, piece], recv_sem=x_recv.at[way, piece],
            device_id={"row": r_to[way]}, device_id_type=MESH)

    def p_copy(pair, part):
        here = pl.ds(part * TILE_ROWS, TILE_ROWS)
        return pltpu.make_async_remote_copy(
            src_ref=oth.at[pair, here], dst_ref=pair_in.at[pair, here], send_sem=p_send.at[pair, part],
            recv_sem=p_recv.at[pair, part], device_id={"depth": partner}, device_id_type=MESH)

    def r_copy(pair, part):
        here = pl.ds(part * TILE_ROWS, TILE_ROWS)
        return pltpu.make_async_remote_copy(
            src_ref=own.at[pair, here], dst_ref=red.at[pair, here], send_sem=r_send.at[pair, part],
            recv_sem=r_recv.at[pair, part], device_id={"depth": tile_of(pair, 1)}, device_id_type=MESH)

    def f_copy(which, sender, kind):
        side = jnp.where(core == which, 1, 0)
        place = pl.ds(pl.multiple_of(sender * 2 * BS, 2 * BS), 2 * BS)
        src, dst = (x_far, x_far_in.at[:, place]) if kind == 0 else (s_buf.at[4 + side, far], s_far_in.at[place])
        return pltpu.make_async_remote_copy(
            src_ref=src, dst_ref=dst, send_sem=f_send.at[kind, which], recv_sem=f_recv.at[kind, sender],
            device_id={"depth": beside[which]}, device_id_type=MESH)

    started = []

    def start(copy):
        copy.start()
        started.append(copy)

    def advance(pair, hop):
        for side in range(2):
            for way in range(2):
                if hop > 1:
                    s_copy(way, pair, side, hop - 1).wait_recv()
                if hop <= half_ring:
                    start(s_copy(way, pair, side, hop))

    parts = panel_rows // TILE_ROWS
    last = chips - 1
    late_from = chips - 2

    def stage(pair, block):
        for side in range(2):
            for i in range(2):
                cur[side, 2 * block + i] = s_buf[2 * pair + side, block, pl.ds(i * BS, BS), :]

    def pick(pair):
        for back in range(ring):
            if pair >= late_from and back == half_ring:
                for side in range(2):
                    for i in range(2):
                        cur[side, 2 * far + i] = jnp.zeros((BS, BS), cur.dtype)
            else:
                stage(pair, lax.rem(z + back, ring))
        for a in range(width_x):
            at = pos[a]
            for side in range(2):
                sel[a * BS:(a + 1) * BS, side * BS:(side + 1) * BS] = cur[side, at]

    def dot(pair, part, count):
        here = pl.ds(part * TILE_ROWS, count * TILE_ROWS)
        value = jnp.dot(x_buf[here, :], sel[...], preferred_element_type=jnp.float32)
        oth[pair, here, :] = value[:, :BS]
        if pair != last:
            for k in range(part, part + count):
                start(p_copy(pair, k))
        own[pair, here, :] = value[:, BS:]

    def late():
        rows_far = jnp.concatenate([s_buf[2 * last, far], s_buf[2 * last + 1, far]], axis=1)
        for part in range(parts):
            here = pl.ds(part * TILE_ROWS, TILE_ROWS)
            value = jnp.dot(x_far[here, :], rows_far, preferred_element_type=jnp.float32)
            oth[last, here, :] = oth[last, here, :] + value[:, :BS]
            start(p_copy(last, part))
            own[last, here, :] = own[last, here, :] + value[:, BS:]

    def pass_on():
        for which in range(2):
            start(f_copy(which, core, 1))

    def gather():
        for part in range(parts):
            here = pl.ds(part * TILE_ROWS, TILE_ROWS)
            value = own[last, here, :]
            for pair in range(last - 1):
                r_copy(pair, part).wait_recv()
                value = value + red[pair, here, :]
            own[last, here, :] = value

    def take():
        for kind in range(2):
            for sender in range(2):
                f_copy(0, sender, kind).wait_recv()
        for part in range(0, parts, 2):
            here = pl.ds(part * TILE_ROWS, 2 * TILE_ROWS)
            value = jnp.dot(x_far_in[here, :], s_far_in[...], preferred_element_type=jnp.float32)
            own[last, here, :] = own[last, here, :] + value

    def share(pair, first, count):
        for part in range(first, first + count):
            here = pl.ds(part * TILE_ROWS, TILE_ROWS)
            p_copy(pair, part).wait_recv()
            own[pair, here, :] = own[pair, here, :] + pair_in[pair, here, :]
            start(r_copy(pair, part))

    def finish():
        for part in range(parts):
            r_copy(last - 1, part).wait_recv()
            p_copy(last, part).wait_recv()
            for i in range(part * TILE_ROWS // BS, (part + 1) * TILE_ROWS // BS):
                here = pl.ds(i * BS, BS)
                value = own[last, here, :] + pair_in[last, here, :]
                value = value + red[last - 1, here, :]
                out[here, :] = jnp.where(mask[i] > 0, value, 0.0).astype(out.dtype)

    def x_forward():
        for way in range(2):
            x_copy(way, 0).wait_recv()
            start(x_copy(way, 2))

    def x_ready():
        for way in range(2):
            for piece in (1, 2):
                x_copy(way, piece).wait_recv()
        for a in range(width_x):
            x_split[a] = x_buf[:, a * BS:(a + 1) * BS]
        x_split[width_x] = jnp.zeros((panel_rows, BS), x_split.dtype)
        for i in range(2):
            x_far[:, i * BS:(i + 1) * BS] = x_split[pos_far[i]]
        for which in range(2):
            start(f_copy(which, core, 0))

    local_copies = [pltpu.make_async_copy(
        x_in, x_buf.at[:, pl.ds(pl.multiple_of(r * quarter, quarter), quarter)], local_sem.at[0])]
    for pair in range(chips):
        for side in range(2):
            local_copies.append(pltpu.make_async_copy(
                s_in.at[:, columns(pair, side)], s_buf.at[2 * pair + side, z], local_sem.at[1 + 2 * pair + side]))

    for k, (src, dst) in enumerate(((cols_in, cols), (rows_in, rows), (mask_in, mask))):
        local_copies.append(pltpu.make_async_copy(src, dst, local_sem.at[1 + deep + k]))

    def find(a, carry):
        wanted = cols[a]
        at = jnp.int32(width_s)
        for q in range(width_s):
            at = jnp.where(rows[q] == wanted, jnp.int32(q), at)
        pos[a] = at
        return carry

    def find_far(i, carry):
        wanted = rows[2 * far + i]
        at = jnp.int32(width_x)
        for a in range(width_x):
            at = jnp.where(cols[a] == wanted, jnp.int32(a), at)
        pos_far[i] = at
        return carry

    order = send_order()
    for pair, hop in order[:1]:
        advance(pair, hop)
    for way in range(2):
        start(x_copy(way, 0))
    for pair, hop in order[1:chips]:
        advance(pair, hop)
    for way in range(2):
        start(x_copy(way, 1))
    for copy in local_copies:
        copy.start()
    for side in range(2):
        cur[side, width_s] = jnp.zeros((BS, BS), cur.dtype)
    for copy in local_copies:
        copy.wait()
    lax.fori_loop(0, width_x, find, 0)
    lax.fori_loop(0, 2, find_far, 0)

    steps = {"x_forward": x_forward, "x_ready": x_ready, "pick": pick, "dot": dot, "share": share, "late": late, "pass": pass_on,
             "take": take, "gather": gather, "finish": finish,
             "land": lambda pair: advance(pair, half_ring + 1)}
    for pair, hop in order[chips:]:
        advance(pair, hop)
        for item in WORK.get((pair, hop), []):
            name, *numbers = item.split()
            steps[name](*map(int, numbers))
    for copy in started:
        copy.wait_send()


def on_device(sizes, x_blocks, cols_x, s_blocks, rows_s, keep_mask):
    ring, wide, deep = sizes
    panel_rows, quarter = x_blocks.shape[0], x_blocks.shape[2]
    own_rows, kept = s_blocks.shape[1], s_blocks.shape[3]
    width_x, width_s = cols_x.shape[2], rows_s.shape[2]
    chips = deep // 2
    parts = panel_rows // TILE_ROWS
    dma = pltpu.SemaphoreType.DMA
    anywhere = pl.BlockSpec(memory_space=pl.ANY)
    result = pl.pallas_call(
        functools.partial(kernel, sizes),
        out_shape=jax.ShapeDtypeStruct((panel_rows, BS), jnp.bfloat16),
        in_specs=[anywhere] * 5,
        out_specs=pl.BlockSpec(memory_space=pltpu.VMEM),
        scratch_shapes=[
            pltpu.SMEM((width_x,), jnp.int32),
            pltpu.SMEM((width_s,), jnp.int32),
            pltpu.SMEM((keep_mask.shape[0],), jnp.int32),
            pltpu.VMEM((deep, ring, own_rows, BS), jnp.bfloat16),
            pltpu.VMEM((panel_rows, quarter * wide), jnp.bfloat16),
            pltpu.VMEM((width_x + 1, panel_rows, BS), jnp.bfloat16),
            pltpu.VMEM((panel_rows, 2 * BS), jnp.bfloat16),
            pltpu.VMEM((panel_rows, 4 * BS), jnp.bfloat16),
            pltpu.VMEM((4 * BS, BS), jnp.bfloat16),
            pltpu.VMEM((2, width_s + 1, BS, BS), jnp.bfloat16),
            pltpu.VMEM((width_x * BS, 2 * BS), jnp.bfloat16),
            pltpu.VMEM((chips, panel_rows, BS), jnp.float32),
            pltpu.VMEM((chips, panel_rows, BS), jnp.float32),
            pltpu.VMEM((chips, panel_rows, BS), jnp.float32),
            pltpu.VMEM((chips - 1, panel_rows, BS), jnp.float32),
            pltpu.SMEM((width_x,), jnp.int32),
            pltpu.SMEM((2,), jnp.int32),
            dma((4 + deep,)),
            dma((2, deep, ring // 2)),
            dma((2, deep, ring // 2)),
            dma((2, 3)),
            dma((2, 3)),
            dma((chips, parts)),
            dma((chips, parts)),
            dma((chips - 1, parts)),
            dma((chips - 1, parts)),
            dma((2, 2)),
            dma((2, 2)),
        ],
        compiler_params=pltpu.CompilerParams(collective_id=0, has_side_effects=True, vmem_limit_bytes=213 << 18),
    )(
        x_blocks.reshape(panel_rows, quarter),
        s_blocks.reshape(own_rows, kept),
        cols_x.reshape(width_x),
        rows_s.reshape(width_s),
        keep_mask.reshape(keep_mask.shape[0]),
    )
    return result.reshape(panel_rows, 1, BS)


def solution(mesh):
    sizes = (mesh.shape["col"], mesh.shape["row"], mesh.shape["depth"])
    placed = (
        P("col", "depth", "row"),
        P("col", "depth", None),
        P("depth", "col", "row", None),
        P("depth", "row", None),
        P("col", "row", "depth"),
    )
    return jax.shard_map(
        functools.partial(on_device, sizes), mesh=mesh, in_specs=placed, out_specs=P("col", "row", "depth"), check_vma=False
    )
```

```python
import functools

import jax
import jax.numpy as jnp
from jax import lax
from jax.experimental import pallas as pl
from jax.experimental.pallas import tpu as pltpu
from jax.sharding import PartitionSpec as P

BS = 128
TILE_ROWS = 256
TRAIL = 1
MESH = pl.DeviceIdType.MESH


def send_order():
    order = [(pair, 1) for pair in range(4)]
    for hop in range(2, 9 - TRAIL):
        order += [(0, hop), (1, hop)]
    for hop in range(2, 2 + TRAIL):
        order += [(0, hop + 7 - TRAIL), (1, hop + 7 - TRAIL), (2, hop)]
    for hop in range(2 + TRAIL, 9):
        order += [(2, hop), (3, hop - TRAIL)]
    order += [(3, hop) for hop in range(9 - TRAIL, 9)]
    return order


WORK = {
    (1, 4): ["x_forward"],
    (1, 7): ["x_ready"],
    (3, 2): ["land 0", "pick 0", "dot 0 0 2"],
    (2, 4): ["dot 0 2 2"],
    (3, 3): ["land 1", "pick 1", "dot 1 0 2"],
    (2, 5): ["dot 1 2 2", "share 0 0 4"],
    (3, 4): ["share 1 0 4"],
    (2, 8): ["pick 2", "dot 2 0 4"],
    (3, 7): ["share 2 0 2", "land 2", "pass", "share 2 2 2"],
    (3, 8): ["pick 3", "dot 3 0 4", "gather", "land 3", "late", "take", "finish"],
}


def kernel(sizes, x_in, s_in, cols_in, rows_in, mask_in, out, cols, rows, mask, s_buf, x_buf, x_split, x_far, x_far_in, s_far_in, cur, sel, oth, own, pair_in,
           red, pos, pos_far,           local_sem, s_send, s_recv, x_send, x_recv, p_send, p_recv, r_send, r_recv,
           f_send, f_recv):
    ring, wide, deep = sizes
    half_ring = ring // 2
    width_x, width_s = cols.shape[0], rows.shape[0]
    chips = deep // 2
    panel_rows = x_buf.shape[0]
    z, r, d = lax.axis_index("col"), lax.axis_index("row"), lax.axis_index("depth")
    y, core = lax.div(d, 2), lax.rem(d, 2)
    quarter = x_in.shape[1]
    half = quarter // 2
    z_to = (lax.rem(z + 1, ring), lax.rem(z + ring - 1, ring))
    r_to = (lax.rem(r + 1, wide), lax.rem(r + wide - 1, wide))
    partner = 2 * y + 1 - core
    far = lax.rem(z + half_ring, ring)

    barrier = pltpu.get_barrier_semaphore()
    friends = [{"col": z_to[0]}, {"col": z_to[1]}, {"row": r_to[0]}, {"row": r_to[1]}, {"depth": partner}]
    friends += [{"depth": 2 * lax.rem(y + j, chips) + core} for j in range(1, chips)]
    beside = (2 * lax.rem(y + 1, chips), 2 * lax.rem(y + chips - 1, chips) + 1)
    friends.append({"depth": jnp.where(core == 0, beside[1], beside[0])})
    for friend in friends:
        pl.semaphore_signal(barrier, inc=1, device_id=friend, device_id_type=MESH)
    pl.semaphore_wait(barrier, len(friends))

    def tile_of(pair, side):
        which = core if side else 1 - core
        step = (2, 3 - 2 * which, 1 + 2 * which, 0)[pair]
        return 2 * lax.rem(y + step, chips) + which

    def columns(pair, side):
        return pl.ds(pl.multiple_of(tile_of(pair, side) * BS, BS), BS)

    def s_copy(way, pair, side, hop):
        back = (hop - 1) if way == 1 else (ring - hop + 1)
        block = lax.rem(z + back, ring)
        tile = 2 * pair + side
        dst = s_buf.at[tile, block]
        src = s_in.at[:, columns(pair, side)] if hop == 1 else dst
        if hop == half_ring:
            src, dst = src.at[pl.ds(way * BS, BS)], dst.at[pl.ds(way * BS, BS)]
        return pltpu.make_async_remote_copy(
            src_ref=src, dst_ref=dst, send_sem=s_send.at[way, tile, hop - 1], recv_sem=s_recv.at[way, tile, hop - 1],
            device_id={"col": z_to[way]}, device_id_type=MESH)

    def x_copy(way, piece):
        if piece < 2:
            part = piece if way == 0 else 1 - piece
            owner = r
        else:
            part = way
            owner = r_to[1 - way]
        dst = x_buf.at[:, pl.ds(pl.multiple_of(owner * quarter + part * half, half), half)]
        src = x_in.at[:, pl.ds(part * half, half)] if piece < 2 else dst
        return pltpu.make_async_remote_copy(
            src_ref=src, dst_ref=dst, send_sem=x_send.at[way, piece], recv_sem=x_recv.at[way, piece],
            device_id={"row": r_to[way]}, device_id_type=MESH)

    def p_copy(pair, part):
        here = pl.ds(part * TILE_ROWS, TILE_ROWS)
        return pltpu.make_async_remote_copy(
            src_ref=oth.at[pair, here], dst_ref=pair_in.at[pair, here], send_sem=p_send.at[pair, part],
            recv_sem=p_recv.at[pair, part], device_id={"depth": partner}, device_id_type=MESH)

    def r_copy(pair, part):
        here = pl.ds(part * TILE_ROWS, TILE_ROWS)
        return pltpu.make_async_remote_copy(
            src_ref=own.at[pair, here], dst_ref=red.at[pair, here], send_sem=r_send.at[pair, part],
            recv_sem=r_recv.at[pair, part], device_id={"depth": tile_of(pair, 1)}, device_id_type=MESH)

    def f_copy(which, sender, kind):
        side = jnp.where(core == which, 1, 0)
        place = pl.ds(pl.multiple_of(sender * 2 * BS, 2 * BS), 2 * BS)
        src, dst = (x_far, x_far_in.at[:, place]) if kind == 0 else (s_buf.at[4 + side, far], s_far_in.at[place])
        return pltpu.make_async_remote_copy(
            src_ref=src, dst_ref=dst, send_sem=f_send.at[kind, which], recv_sem=f_recv.at[kind, sender],
            device_id={"depth": beside[which]}, device_id_type=MESH)

    started = []

    def start(copy):
        copy.start()
        started.append(copy)

    def advance(pair, hop):
        for side in range(2):
            for way in range(2):
                if hop > 1:
                    s_copy(way, pair, side, hop - 1).wait_recv()
                if hop <= half_ring:
                    start(s_copy(way, pair, side, hop))

    parts = panel_rows // TILE_ROWS
    last = chips - 1
    late_from = chips - 2

    def stage(pair, block):
        for side in range(2):
            for i in range(2):
                cur[side, 2 * block + i] = s_buf[2 * pair + side, block, pl.ds(i * BS, BS), :]

    def pick(pair):
        for back in range(ring):
            if pair >= late_from and back == half_ring:
                for side in range(2):
                    for i in range(2):
                        cur[side, 2 * far + i] = jnp.zeros((BS, BS), cur.dtype)
            else:
                stage(pair, lax.rem(z + back, ring))
        for a in range(width_x):
            at = pos[a]
            for side in range(2):
                sel[a * BS:(a + 1) * BS, side * BS:(side + 1) * BS] = cur[side, at]

    def dot(pair, part, count):
        here = pl.ds(part * TILE_ROWS, count * TILE_ROWS)
        value = jnp.dot(x_buf[here, :], sel[...], preferred_element_type=jnp.float32)
        oth[pair, here, :] = value[:, :BS]
        if pair != last:
            for k in range(part, part + count):
                start(p_copy(pair, k))
        own[pair, here, :] = value[:, BS:]

    def late():
        rows_far = jnp.concatenate([s_buf[2 * last, far], s_buf[2 * last + 1, far]], axis=1)
        for part in range(parts):
            here = pl.ds(part * TILE_ROWS, TILE_ROWS)
            value = jnp.dot(x_far[here, :], rows_far, preferred_element_type=jnp.float32)
            oth[last, here, :] = oth[last, here, :] + value[:, :BS]
            start(p_copy(last, part))
            own[last, here, :] = own[last, here, :] + value[:, BS:]

    def pass_on():
        for which in range(2):
            start(f_copy(which, core, 1))

    def gather():
        for part in range(parts):
            here = pl.ds(part * TILE_ROWS, TILE_ROWS)
            value = own[last, here, :]
            for pair in range(last - 1):
                r_copy(pair, part).wait_recv()
                value = value + red[pair, here, :]
            own[last, here, :] = value

    def take():
        for kind in range(2):
            for sender in range(2):
                f_copy(0, sender, kind).wait_recv()
        for part in range(0, parts, 2):
            here = pl.ds(part * TILE_ROWS, 2 * TILE_ROWS)
            value = jnp.dot(x_far_in[here, :], s_far_in[...], preferred_element_type=jnp.float32)
            own[last, here, :] = own[last, here, :] + value

    def share(pair, first, count):
        for part in range(first, first + count):
            here = pl.ds(part * TILE_ROWS, TILE_ROWS)
            p_copy(pair, part).wait_recv()
            own[pair, here, :] = own[pair, here, :] + pair_in[pair, here, :]
            start(r_copy(pair, part))

    def finish():
        for part in range(parts):
            r_copy(last - 1, part).wait_recv()
            p_copy(last, part).wait_recv()
            for i in range(part * TILE_ROWS // BS, (part + 1) * TILE_ROWS // BS):
                here = pl.ds(i * BS, BS)
                value = own[last, here, :] + pair_in[last, here, :]
                value = value + red[last - 1, here, :]
                out[here, :] = jnp.where(mask[i] > 0, value, 0.0).astype(out.dtype)

    def x_forward():
        for way in range(2):
            x_copy(way, 0).wait_recv()
            start(x_copy(way, 2))

    def x_ready():
        for way in range(2):
            for piece in (1, 2):
                x_copy(way, piece).wait_recv()
        for a in range(width_x):
            x_split[a] = x_buf[:, a * BS:(a + 1) * BS]
        x_split[width_x] = jnp.zeros((panel_rows, BS), x_split.dtype)
        for i in range(2):
            x_far[:, i * BS:(i + 1) * BS] = x_split[pos_far[i]]
        for which in range(2):
            start(f_copy(which, core, 0))

    local_copies = [pltpu.make_async_copy(
        x_in, x_buf.at[:, pl.ds(pl.multiple_of(r * quarter, quarter), quarter)], local_sem.at[0])]
    for pair in range(chips):
        for side in range(2):
            local_copies.append(pltpu.make_async_copy(
                s_in.at[:, columns(pair, side)], s_buf.at[2 * pair + side, z], local_sem.at[1 + 2 * pair + side]))

    for k, (src, dst) in enumerate(((cols_in, cols), (rows_in, rows), (mask_in, mask))):
        local_copies.append(pltpu.make_async_copy(src, dst, local_sem.at[1 + deep + k]))

    def find(a, carry):
        wanted = cols[a]
        at = jnp.int32(width_s)
        for q in range(width_s):
            at = jnp.where(rows[q] == wanted, jnp.int32(q), at)
        pos[a] = at
        return carry

    def find_far(i, carry):
        wanted = rows[2 * far + i]
        at = jnp.int32(width_x)
        for a in range(width_x):
            at = jnp.where(cols[a] == wanted, jnp.int32(a), at)
        pos_far[i] = at
        return carry

    order = send_order()
    for pair, hop in order[:1]:
        advance(pair, hop)
    for way in range(2):
        start(x_copy(way, 0))
    for pair, hop in order[1:chips]:
        advance(pair, hop)
    for way in range(2):
        start(x_copy(way, 1))
    for copy in local_copies:
        copy.start()
    for side in range(2):
        cur[side, width_s] = jnp.zeros((BS, BS), cur.dtype)
    for copy in local_copies:
        copy.wait()
    lax.fori_loop(0, width_x, find, 0)
    lax.fori_loop(0, 2, find_far, 0)

    steps = {"x_forward": x_forward, "x_ready": x_ready, "pick": pick, "dot": dot, "share": share, "late": late, "pass": pass_on,
             "take": take, "gather": gather, "finish": finish,
             "land": lambda pair: advance(pair, half_ring + 1)}
    for pair, hop in order[chips:]:
        advance(pair, hop)
        for item in WORK.get((pair, hop), []):
            name, *numbers = item.split()
            steps[name](*map(int, numbers))
    for copy in started:
        copy.wait_send()


def on_device(sizes, x_blocks, cols_x, s_blocks, rows_s, keep_mask):
    ring, wide, deep = sizes
    panel_rows, quarter = x_blocks.shape[0], x_blocks.shape[2]
    own_rows, kept = s_blocks.shape[1], s_blocks.shape[3]
    width_x, width_s = cols_x.shape[2], rows_s.shape[2]
    chips = deep // 2
    parts = panel_rows // TILE_ROWS
    dma = pltpu.SemaphoreType.DMA
    anywhere = pl.BlockSpec(memory_space=pl.ANY)
    result = pl.pallas_call(
        functools.partial(kernel, sizes),
        out_shape=jax.ShapeDtypeStruct((panel_rows, BS), jnp.bfloat16),
        in_specs=[anywhere] * 5,
        out_specs=pl.BlockSpec(memory_space=pltpu.VMEM),
        scratch_shapes=[
            pltpu.SMEM((width_x,), jnp.int32),
            pltpu.SMEM((width_s,), jnp.int32),
            pltpu.SMEM((keep_mask.shape[0],), jnp.int32),
            pltpu.VMEM((deep, ring, own_rows, BS), jnp.bfloat16),
            pltpu.VMEM((panel_rows, quarter * wide), jnp.bfloat16),
            pltpu.VMEM((width_x + 1, panel_rows, BS), jnp.bfloat16),
            pltpu.VMEM((panel_rows, 2 * BS), jnp.bfloat16),
            pltpu.VMEM((panel_rows, 4 * BS), jnp.bfloat16),
            pltpu.VMEM((4 * BS, BS), jnp.bfloat16),
            pltpu.VMEM((2, width_s + 1, BS, BS), jnp.bfloat16),
            pltpu.VMEM((width_x * BS, 2 * BS), jnp.bfloat16),
            pltpu.VMEM((chips, panel_rows, BS), jnp.float32),
            pltpu.VMEM((chips, panel_rows, BS), jnp.float32),
            pltpu.VMEM((chips, panel_rows, BS), jnp.float32),
            pltpu.VMEM((chips - 1, panel_rows, BS), jnp.float32),
            pltpu.SMEM((width_x,), jnp.int32),
            pltpu.SMEM((2,), jnp.int32),
            dma((4 + deep,)),
            dma((2, deep, ring // 2)),
            dma((2, deep, ring // 2)),
            dma((2, 3)),
            dma((2, 3)),
            dma((chips, parts)),
            dma((chips, parts)),
            dma((chips - 1, parts)),
            dma((chips - 1, parts)),
            dma((2, 2)),
            dma((2, 2)),
        ],
        compiler_params=pltpu.CompilerParams(collective_id=0, has_side_effects=True, vmem_limit_bytes=213 << 18),
    )(
        x_blocks.reshape(panel_rows, quarter),
        s_blocks.reshape(own_rows, kept),
        cols_x.reshape(width_x),
        rows_s.reshape(width_s),
        keep_mask.reshape(keep_mask.shape[0]),
    )
    return result.reshape(panel_rows, 1, BS)


def solution(mesh):
    sizes = (mesh.shape["col"], mesh.shape["row"], mesh.shape["depth"])
    placed = (
        P("col", "depth", "row"),
        P("col", "depth", None),
        P("depth", "col", "row", None),
        P("depth", "row", None),
        P("col", "row", "depth"),
    )
    return jax.shard_map(
        functools.partial(on_device, sizes), mesh=mesh, in_specs=placed, out_specs=P("col", "row", "depth"), check_vma=False
    )
```
